256 devices in a mesh: row: 4 (over x), col: 8 (over z_lo, core), depth: 8 (over z_hi, y).
Axes of the slice: x: 4, y: 4, z: 8 (z_hi: 2, z_lo: 4; z = z_hi * 4 + z_lo), core: 2. Of those that a mesh axis runs over, the one named last changes fastest.
Arguments:
- left_panel: float32 [8192, 2048], P(('row', 'col'), 'depth'), may hold values from -1 to 1
- upper_inverse: float32 [2048, 2048], P(None, 'depth'), as said below
- lower_inverse: float32 [2048, 2048], P('depth'), as said below
- top_panel: float32 [2048, 8192], P('depth', 'col'), may hold values from -1 to 1
- trailing: float32 [8192, 8192], P('row', ('col', 'depth')), may hold values from -6 to 6
Outputs:
- schur_block: float32 [8192, 8192], P('row', ('col', 'depth'))
The draws below stay inside these ranges and needn't reach their ends.
Inputs may be any that keep to these rules, and one draw needn't show every extreme that they name: `upper_inverse`: zero below the diagonal. `lower_inverse`: zero above the diagonal.
All inputs are finite; a program needn't handle non-finite values.
Results may differ from the reference program's by a relative error of at most 0.00005.
Values sent between devices are 32-bit elements; how exact they have to be, the bound alone decides.
A program may use at most 128 MiB of HBM per device.

```python
import jax
import jax.numpy as jnp
from jax import lax

ORDER = 8192
PANEL = 2048
WINDOW = 8192


def triangle_draw(key, upper):
    key_off, key_diag = jax.random.split(key)
    scale = PANEL ** (-0.5)
    off_values = jnp.clip(jax.random.normal(key_off, (PANEL, PANEL), jnp.float32), -4.0, 4.0) * scale
    diag_values = jax.random.uniform(key_diag, (PANEL, PANEL), jnp.float32, 1.0, 1.8)
    first = lax.broadcasted_iota(jnp.int32, (PANEL, PANEL), 0)
    second = lax.broadcasted_iota(jnp.int32, (PANEL, PANEL), 1)
    keep = second > first if upper else second < first
    return jnp.where(keep, off_values, jnp.where(first == second, diag_values, 0.0)).astype(jnp.float32)


def draw_upper_inverse(key, part):
    key = jax.random.fold_in(key, 11)
    return triangle_draw(key, True)


def draw_lower_inverse(key, part):
    key = jax.random.fold_in(key, 23)
    return triangle_draw(key, False)


def levels(stream_key, extent, shards, smallest, largest):
    factor_of = 1.0
    for position, blocks in shards:
        draws = jax.random.uniform(jax.random.fold_in(jax.random.fold_in(stream_key, 6), position), (blocks,), jnp.float32, smallest / len(shards), largest / len(shards))
        factor_of = factor_of * jnp.repeat(jnp.exp(draws), extent[position] // blocks).reshape((-1,) + (1,) * (len(extent) - 1 - position))
    return factor_of


def gaussian(own_key, extent, width, limit, cuts=(), kind=jnp.bfloat16):
    result = width * jax.random.normal(own_key, extent, jnp.float32)
    if cuts:
        result = result * levels(own_key, extent, cuts, -0.22, 0.18)
    return jnp.clip(result, -limit, limit).astype(kind)


def setup_inputs(seed: int = 0) -> dict:
    seeds = jax.random.split(jax.random.key(seed), 6)
    return {
        "left_panel": gaussian(seeds[0], (WINDOW, PANEL), 0.15, 1.0, ((0, 32), (1, 8)), jnp.float32),
        "upper_inverse": draw_upper_inverse(jax.random.fold_in(seeds[5], 71), 0),
        "lower_inverse": draw_lower_inverse(jax.random.fold_in(seeds[5], 71), 0),
        "top_panel": gaussian(seeds[3], (PANEL, ORDER), 0.15, 1.0, ((0, 8), (1, 8)), jnp.float32),
        "trailing": gaussian(seeds[4], (WINDOW, ORDER), 1.0, 6.0, ((0, 4), (1, 64)), jnp.float32),
    }


def reference(left_panel, upper_inverse, lower_inverse, top_panel, trailing):
    solved_left = jnp.dot(left_panel, upper_inverse, precision=lax.Precision.HIGHEST, preferred_element_type=jnp.float32)
    solved_top = jnp.dot(lower_inverse, top_panel, precision=lax.Precision.HIGHEST, preferred_element_type=jnp.float32)
    update = jnp.dot(solved_left, solved_top, precision=lax.Precision.HIGHEST, preferred_element_type=jnp.float32)
    return trailing - update
```

```python
import functools

import jax
import jax.numpy as jnp
from jax import lax
from jax.experimental import pallas as pl
from jax.experimental.pallas import tpu as pltpu
from jax.sharding import PartitionSpec as P

MESH = pl.DeviceIdType.MESH
F32 = jnp.float32
BF16 = jnp.bfloat16
B = 256


def split(v):
    high = v.astype(BF16)
    return high, (v - high.astype(F32)).astype(BF16)


def mm3(a, b):
    (ah, al), (bh, bl) = a, b
    dot = functools.partial(jnp.dot, preferred_element_type=F32)
    return dot(ah, bh) + (dot(ah, bl) + dot(al, bh))


def kernel(
    left, upper, lower, top, trailing, out,
    gbuf, ubuf, lbuf, sbuf, tloc, tbuf, th, tl, pbuf, rbuf,
    gsem, xsend, gsend, fsem, fsend, tsem, tsend, rsem, rsend, csem, csend, psem, psend,
):
    x = lax.axis_index("row")
    c = lax.axis_index("col")
    d = lax.axis_index("depth")
    k = lax.rem(c, 2)
    zl = c // 2
    y = lax.rem(d, 4)
    zh = d // 4
    z = zh * 4 + zl
    d2 = (1 - zh) * 4 + y

    def dev(x_, y_, z_, k_):
        return (x_, lax.rem(z_, 4) * 2 + k_, (z_ // 4) * 4 + y_)

    def rot4(v, by):
        return lax.rem(v + by, 4)

    def rot8(v, by):
        return lax.rem(v + by + 8, 8)

    def remote(src, dst, ss, rs, device):
        return pltpu.make_async_remote_copy(
            src_ref=src, dst_ref=dst, send_sem=ss, recv_sem=rs, device_id=device, device_id_type=MESH
        )

    def landed(ref, sem):
        pltpu.make_async_copy(ref, ref, sem).wait()

    zo = rot8(z, 4)
    z_up, z_down = rot8(z, 1), rot8(z, -1)

    peers = [dev(x, y, z, 1 - k), dev(x, y, zo, 0), dev(x, y, zo, 1), dev(x, y, z_up, k), dev(x, y, z_down, k)]
    peers += [dev(x, rot4(y, i), z, k) for i in (1, 2, 3)]
    peers += [dev(rot4(x, i), y, z, j) for i in (1, 2, 3) for j in (0, 1)]
    barrier = pltpu.get_barrier_semaphore()
    for peer in peers:
        pl.semaphore_signal(barrier, inc=1, device_id=peer, device_id_type=MESH)
    pl.semaphore_wait(barrier, len(peers))

    sends = []

    def start(cp, when=None):
        if when is None:
            cp.start()
        else:
            pl.when(when)(lambda: cp.start())
        sends.append((cp, when))

    is_self = jnp.logical_and(k == 0, zh == 0)
    start(
        remote(left, gbuf.at[d], xsend.at[0], gsem.at[d], dev(x, y, k * 4 + zl, 0)),
        jnp.logical_not(is_self),
    )
    pl.when(is_self)(lambda: pltpu.make_async_copy(left, gbuf.at[d], gsem.at[d]).start())

    mine = k == x // 2
    for h in (0, 1):
        block = top.at[:, pl.ds(pl.multiple_of(h * 512 + lax.rem(x, 2) * B, B), B)]
        own = jnp.logical_and(k == 1, zh == h)
        start(
            remote(block, gbuf.at[d], xsend.at[1 + h], gsem.at[d], dev(x, y, h * 4 + zl, 1)),
            jnp.logical_and(mine, jnp.logical_not(own)),
        )
        pl.when(jnp.logical_and(mine, own))(
            lambda: pltpu.make_async_copy(block, gbuf.at[d], gsem.at[d]).start()
        )

    edge = jnp.logical_or(zl == 0, zl == 3)
    z_cross = jnp.where(zl == 0, z_down, z_up)
    z_in = jnp.where(zl == 0, z_up, z_down)
    uq = upper.at[pl.ds(pl.multiple_of(x * 512, 512), 512), :]
    lq = lower.at[:, pl.ds(pl.multiple_of(x * 512, 512), 512)]
    is0, is1 = k == 0, k == 1
    for is_k, src, buf in ((is0, uq, ubuf), (is1, lq, lbuf)):
        start(
            remote(src, buf.at[x], fsend.at[0], fsem.at[x], dev(x, y, z_cross, k)),
            jnp.logical_and(edge, is_k),
        )

    def gather_y(slot, j):
        for i in (1, 2, 3):
            yy = rot4(y, i)
            start(
                remote(gbuf.at[slot], gbuf.at[slot], gsend.at[j, i - 1], gsem.at[slot], dev(x, yy, z, k)),
                jnp.logical_or(slot < 4, yy > y),
            )

    landed(gbuf.at[d], gsem.at[d])
    gather_y(d, 0)
    landed(ubuf.at[0], fsem.at[x])
    for is_k, buf in ((is0, ubuf), (is1, lbuf)):
        start(
            remote(buf.at[x], buf.at[x], fsend.at[1], fsem.at[x], dev(x, y, z_in, k)),
            jnp.logical_and(edge, is_k),
        )
        for i in (1, 2, 3):
            start(
                remote(buf.at[x], buf.at[x], fsend.at[1 + i], fsem.at[x], dev(rot4(x, i), y, z, k)),
                is_k,
            )
    landed(gbuf.at[d2], gsem.at[d2])
    gather_y(d2, 1)

    def wait_block(i):
        other_y = lax.rem(i, 4) != y

        @pl.when(jnp.logical_and(other_y, i <= 4 + y))
        def _():
            landed(gbuf.at[i], gsem.at[i])

        q = i // 2

        @pl.when(jnp.logical_and(lax.rem(i, 2) == 0, q != x))
        def _():
            landed(ubuf.at[q], fsem.at[q])

    @pl.when(k == 0)
    def _():
        sbuf[z] = jnp.zeros((2, B, B), F32)

        @pl.loop(0, 8)
        def _(i):
            wait_block(i)

            @pl.when(i <= d)
            def _():
                f = upper[pl.ds(pl.multiple_of(i * B, B), B), :]
                sbuf[z, zh] += mm3(split(gbuf[i]), split(f))

            @pl.when(i <= d2)
            def _():
                f = ubuf[i // 2, pl.ds(pl.multiple_of(lax.rem(i, 2) * B, B), B), :]
                sbuf[z, 1 - zh] += mm3(split(gbuf[i]), split(f))

        remote(sbuf.at[z], sbuf.at[z], csend.at[0], csem.at[0], dev(x, y, z, 1)).start()

    t_core = x // 2
    t_slot = lax.rem(x, 2)

    @pl.when(k == 1)
    def _():
        tloc[...] = jnp.zeros((2, B, B), F32)

        @pl.loop(0, 8)
        def _(i):
            wait_block(i)

            @pl.when(i <= d)
            def _():
                f = lower[:, pl.ds(pl.multiple_of(i * B, B), B)]
                tloc[zh] += mm3(split(f), split(gbuf[i]))

            @pl.when(i <= d2)
            def _():
                f = lbuf[i // 2, :, pl.ds(pl.multiple_of(lax.rem(i, 2) * B, B), B)]
                tloc[1 - zh] += mm3(split(f), split(gbuf[i]))

    for i in range(4):
        own = jnp.logical_and(t_core == 1, i == 0)
        start(
            remote(tloc, tbuf.at[t_slot], tsend.at[i], tsem.at[t_slot], dev(rot4(x, i), y, z, t_core)),
            jnp.logical_and(is1, jnp.logical_not(own)),
        )
    pl.when(jnp.logical_and(is1, t_core == 1))(
        lambda: pltpu.make_async_copy(tloc, tbuf.at[t_slot], tsem.at[t_slot]).start()
    )

    def piece(i):
        s = (i + 1) // 2
        return rot8(z, jnp.where(lax.rem(i, 2) == 1, -s, s))

    half = pl.ds(pl.multiple_of(k * 128, 128), 128)
    other_half = pl.ds(pl.multiple_of((1 - k) * 128, 128), 128)

    def ring(p, ss, i, z_):
        r = sbuf.at[p, :, half, :]
        return remote(r, r, ss, rsem.at[i], dev(x, y, z_, k))

    def to_sibling(p, i):
        r = sbuf.at[p, :, half, :]
        return remote(r, r, csend.at[i], csem.at[i], dev(x, y, z, 1 - k))

    def arrive(i):
        p = piece(i)
        landed(sbuf.at[p, :, half, :], rsem.at[i])
        odd = lax.rem(i, 2) == 1
        pl.when(jnp.logical_and(odd, i < 7))(lambda: ring(p, rsend.at[i], i + 2, z_up).start())
        pl.when(jnp.logical_and(jnp.logical_not(odd), i < 6))(lambda: ring(p, rsend.at[i], i + 2, z_down).start())
        to_sibling(p, i).start()

    def rows_of(p):
        return pl.ds(pl.multiple_of((2 * lax.rem(p, 4) + p // 4) * B, B), B)

    def partial_copy(i, j):
        rows = rows_of(piece(i))
        yy = rot4(y, j)
        return remote(pbuf.at[i, yy], rbuf.at[j - 1, rows], psend.at[j - 1, i], psem.at[j - 1, i], dev(x, yy, z, k))

    def process(i):
        p = piece(i)
        rows = rows_of(p)
        a = [split(sbuf[p, n]) for n in (0, 1)]
        for h in (0, 1):
            acc = mm3(a[0], (th[h, 0], tl[h, 0])) + mm3(a[1], (th[h, 1], tl[h, 1]))
            pbuf[i, 2 * h] = acc[:, :128]
            pbuf[i, 2 * h + 1] = acc[:, 128:]
        for j in (1, 2, 3):
            partial_copy(i, j).start()
        out[rows, :] = trailing[rows, :] - pbuf[i, y]

    @pl.when(k == 1)
    def _():
        landed(sbuf.at[z], csem.at[0])

    ring(z, rsend.at[0], 1, z_up).start()
    ring(z, rsend.at[8], 2, z_down).start()

    for h in (0, 1):
        landed(tbuf.at[h], tsem.at[h])
        for n in (0, 1):
            high, low = split(tbuf[h, n])
            th[h, n] = high
            tl[h, n] = low

    process(0)

    @pl.loop(1, 9)
    def _(i):
        pl.when(i < 8)(lambda: arrive(i))

        @pl.when(i > 1)
        def _():
            landed(sbuf.at[piece(i - 1), :, other_half, :], csem.at[i - 1])
            process(i - 1)

    @pl.loop(0, 8)
    def _(i):
        rows = rows_of(piece(i))
        for j in (1, 2, 3):
            landed(rbuf.at[j - 1, rows], psem.at[j - 1, i])
        out[rows, :] = out[rows, :] - ((rbuf[0, rows] + rbuf[1, rows]) + rbuf[2, rows])

    for cp, when in sends:
        if when is None:
            cp.wait_send()
        else:
            pl.when(when)(lambda: cp.wait_send())

    @pl.when(k == 0)
    def _():
        remote(sbuf.at[z], sbuf.at[z], csend.at[0], csem.at[0], dev(x, y, z, 1)).wait_send()

    ring(z, rsend.at[0], 1, z_up).wait_send()
    ring(z, rsend.at[8], 2, z_down).wait_send()

    @pl.loop(1, 8)
    def _(i):
        pl.when(i < 6)(lambda: ring(z, rsend.at[i], i + 2, z_up).wait_send())
        to_sibling(z, i).wait_send()

    @pl.loop(0, 8)
    def _(i):
        for j in (1, 2, 3):
            partial_copy(i, j).wait_send()


def local(left_panel, upper_inverse, lower_inverse, top_panel, trailing):
    vmem = pl.BlockSpec(memory_space=pltpu.VMEM)
    dma = pltpu.SemaphoreType.DMA
    return pl.pallas_call(
        kernel,
        out_shape=jax.ShapeDtypeStruct(trailing.shape, F32),
        in_specs=[vmem] * 5,
        out_specs=vmem,
        scratch_shapes=[
            pltpu.VMEM((8, B, B), F32),
            pltpu.VMEM((4, 512, B), F32),
            pltpu.VMEM((4, B, 512), F32),
            pltpu.VMEM((8, 2, B, B), F32),
            pltpu.VMEM((2, B, B), F32),
            pltpu.VMEM((2, 2, B, B), F32),
            pltpu.VMEM((2, 2, B, B), BF16),
            pltpu.VMEM((2, 2, B, B), BF16),
            pltpu.VMEM((8, 4, B, 128), F32),
            pltpu.VMEM((3, 2048, 128), F32),
            dma((8,)), dma((3,)), dma((2, 3)), dma((4,)), dma((5,)), dma((2,)), dma((4,)),
            dma((8,)), dma((9,)), dma((8,)), dma((8,)), dma((3, 8)), dma((3, 8)),
        ],
        compiler_params=pltpu.CompilerParams(
            collective_id=0, has_side_effects=True, vmem_limit_bytes=56 * 2**20
        ),
        name="schur",
    )(left_panel, upper_inverse, lower_inverse, top_panel, trailing)


def solution(mesh):
    placed = (
        P(("row", "col"), "depth"),
        P(None, "depth"),
        P("depth", None),
        P("depth", "col"),
        P("row", ("col", "depth")),
    )
    return jax.shard_map(
        local, mesh=mesh, in_specs=placed, out_specs=P("row", ("col", "depth")), check_vma=False
    )
```

```python
import functools

import jax
import jax.numpy as jnp
from jax import lax
from jax.experimental import pallas as pl
from jax.experimental.pallas import tpu as pltpu
from jax.sharding import PartitionSpec as P

MESH = pl.DeviceIdType.MESH
F32 = jnp.float32
BF16 = jnp.bfloat16
B = 256


def split(v):
    high = v.astype(BF16)
    return high, (v - high.astype(F32)).astype(BF16)


def mm3(a, b):
    (ah, al), (bh, bl) = a, b
    dot = functools.partial(jnp.dot, preferred_element_type=F32)
    return dot(ah, bh) + (dot(ah, bl) + dot(al, bh))


def kernel(
    left, upper, lower, top, trailing, out,
    gbuf, uown, lown, ubuf, lbuf, sbuf, tloc, tbuf, th, tl, pbuf, rbuf, relay,
    gsem, xsend, gsend, fsem, fsend, tsem, tsend, rsem, rsend, csem, csend,
    esem, esend, psem, psend, lsem,
):
    x = lax.axis_index("row")
    c = lax.axis_index("col")
    d = lax.axis_index("depth")
    k = lax.rem(c, 2)
    zl = c // 2
    y = lax.rem(d, 4)
    zh = d // 4
    z = zh * 4 + zl
    d2 = (1 - zh) * 4 + y

    def dev(x_, y_, z_, k_):
        return (x_, lax.rem(z_, 4) * 2 + k_, (z_ // 4) * 4 + y_)

    def rot4(v, by):
        return lax.rem(v + by + 4, 4)

    def rot8(v, by):
        return lax.rem(v + by + 8, 8)

    def remote(src, dst, ss, rs, device):
        return pltpu.make_async_remote_copy(
            src_ref=src, dst_ref=dst, send_sem=ss, recv_sem=rs, device_id=device, device_id_type=MESH
        )

    def landed(ref, sem):
        pltpu.make_async_copy(ref, ref, sem).wait()

    zo = rot8(z, 4)
    z_up, z_down = rot8(z, 1), rot8(z, -1)
    is0, is1 = k == 0, k == 1

    pl.when(is0)(lambda: pltpu.make_async_copy(upper, uown, lsem.at[0]).start())
    pl.when(is1)(lambda: pltpu.make_async_copy(lower, lown, lsem.at[0]).start())
    pltpu.make_async_copy(trailing, out, lsem.at[1]).start()

    peers = [dev(x, y, z, 1 - k), dev(x, y, zo, 0), dev(x, y, zo, 1), dev(x, y, z_up, k), dev(x, y, z_down, k)]
    peers += [dev(x, rot4(y, i), z, k) for i in (1, 2, 3)]
    peers += [dev(rot4(x, i), y, z, j) for i in (1, 3) for j in (0, 1)]
    barrier = pltpu.get_barrier_semaphore()
    for peer in peers:
        pl.semaphore_signal(barrier, inc=1, device_id=peer, device_id_type=MESH)
    pl.semaphore_wait(barrier, len(peers))

    sends = []

    def start(cp, when=None):
        if when is None:
            cp.start()
        else:
            pl.when(when)(lambda: cp.start())
        sends.append((cp, when))

    is_self = jnp.logical_and(k == 0, zh == 0)
    start(
        remote(left, gbuf.at[d], xsend.at[0], gsem.at[d], dev(x, y, k * 4 + zl, 0)),
        jnp.logical_not(is_self),
    )
    pl.when(is_self)(lambda: pltpu.make_async_copy(left, gbuf.at[d], gsem.at[d]).start())

    mine = k == x // 2
    for h in (0, 1):
        block = top.at[:, pl.ds(pl.multiple_of(h * 512 + lax.rem(x, 2) * B, B), B)]
        own = jnp.logical_and(k == 1, zh == h)
        start(
            remote(block, gbuf.at[d], xsend.at[1 + h], gsem.at[d], dev(x, y, h * 4 + zl, 1)),
            jnp.logical_and(mine, jnp.logical_not(own)),
        )
        pl.when(jnp.logical_and(mine, own))(
            lambda: pltpu.make_async_copy(block, gbuf.at[d], gsem.at[d]).start()
        )

    edge = jnp.logical_or(zl == 0, zl == 3)
    z_cross = jnp.where(zl == 0, z_down, z_up)
    z_in = jnp.where(zl == 0, z_up, z_down)

    def u_share(g, xs, half=None):
        rows = pl.ds(xs * 128, 128) if half is None else pl.ds(xs * 128 + half * 64, 64)
        return ubuf.at[g, rows]

    def l_share(g, xs, half=None):
        rows = pl.ds(xs * 64, 64) if half is None else pl.ds(xs * 64 + half * 32, 32)
        return lbuf.at[g, rows]

    kinds = ((is0, u_share), (is1, l_share))
    for g in range(4):
        uq = upper.at[pl.ds(pl.multiple_of(g * 512 + x * 128, 128), 128), :]
        lq = lower.at[pl.ds(pl.multiple_of(x * 64, 64), 64), pl.ds(g * 512, 512)]
        for (is_k, share), src in zip(kinds, (uq, lq)):
            start(
                remote(src, share(g, x), fsend.at[g, 0], fsem.at[g, x, 0], dev(x, y, z_cross, k)),
                jnp.logical_and(jnp.logical_and(edge, is_k), 2 * g <= d),
            )

    def chunk(g):
        wanted = 2 * g <= d2

        @pl.when(wanted)
        def _():
            landed(u_share(g, x), fsem.at[g, x, 0])

        for is_k, share in kinds:
            go = jnp.logical_and(wanted, is_k)
            r = share(g, x)
            start(
                remote(r, r, fsend.at[g, 1], fsem.at[g, x, 0], dev(x, y, z_in, k)), jnp.logical_and(edge, go)
            )
            start(remote(r, r, fsend.at[g, 2], fsem.at[g, x, 0], dev(rot4(x, 1), y, z, k)), go)
            start(remote(r, r, fsend.at[g, 3], fsem.at[g, x, 0], dev(rot4(x, -1), y, z, k)), go)

    def chunk_relay(g):
        wanted = 2 * g <= d2
        for half, by in ((0, 1), (1, -1)):
            xs = rot4(x, -by)

            @pl.when(wanted)
            def _():
                landed(u_share(g, xs), fsem.at[g, xs, 0])

            for is_k, share in kinds:
                r = share(g, xs, half)
                start(
                    remote(r, r, fsend.at[g, 4 + half], fsem.at[g, xs, half], dev(rot4(x, by), y, z, k)),
                    jnp.logical_and(wanted, is_k),
                )

    def gather_y(slot, j):
        for i in (1, 2, 3):
            yy = rot4(y, i)
            start(
                remote(gbuf.at[slot], gbuf.at[slot], gsend.at[j, i - 1], gsem.at[slot], dev(x, yy, z, k)),
                jnp.logical_or(slot < 4, yy > y),
            )

    landed(gbuf.at[d], gsem.at[d])
    gather_y(d, 0)
    chunk(0)
    landed(gbuf.at[d2], gsem.at[d2])
    gather_y(d2, 1)
    chunk(1)
    chunk_relay(0)
    chunk(2)
    chunk_relay(1)
    chunk(3)
    chunk_relay(2)
    chunk_relay(3)

    landed(uown, lsem.at[0])

    def wait_block(i):
        @pl.when(jnp.logical_and(lax.rem(i, 4) != y, i <= 4 + y))
        def _():
            landed(gbuf.at[i], gsem.at[i])

    def wait_chunk(i):
        g = i // 2
        xs = rot4(x, 2)

        @pl.when(jnp.logical_and(lax.rem(i, 2) == 0, i <= d2))
        def _():
            landed(u_share(g, xs, 0), fsem.at[g, xs, 0])
            landed(u_share(g, xs, 1), fsem.at[g, xs, 1])

    @pl.when(k == 0)
    def _():
        sbuf[z] = jnp.zeros((2, B, B), F32)

        @pl.loop(0, 8)
        def _(i):
            wait_block(i)
            wait_chunk(i)

            @pl.when(i <= d)
            def _():
                f = uown[pl.ds(pl.multiple_of(i * B, B), B), :]
                sbuf[z, zh] += mm3(split(gbuf[i]), split(f))

            @pl.when(i <= d2)
            def _():
                f = ubuf[i // 2, pl.ds(pl.multiple_of(lax.rem(i, 2) * B, B), B), :]
                sbuf[z, 1 - zh] += mm3(split(gbuf[i]), split(f))

        remote(sbuf.at[z], sbuf.at[z], csend.at[0], csem.at[0], dev(x, y, z, 1)).start()

    t_core = x // 2
    t_slot = lax.rem(x, 2)

    @pl.when(k == 1)
    def _():
        tloc[...] = jnp.zeros((2, B, B), F32)

        @pl.loop(0, 8)
        def _(i):
            wait_block(i)
            wait_chunk(i)

            @pl.when(i <= d)
            def _():
                f = lown[:, pl.ds(pl.multiple_of(i * B, B), B)]
                tloc[zh] += mm3(split(f), split(gbuf[i]))

            @pl.when(i <= d2)
            def _():
                f = lbuf[i // 2, :, pl.ds(pl.multiple_of(lax.rem(i, 2) * B, B), B)]
                tloc[1 - zh] += mm3(split(f), split(gbuf[i]))

    for i, by in enumerate((0, 1, -1)):
        own = jnp.logical_and(t_core == 1, i == 0)
        for n in (0, 1):
            start(
                remote(
                    tloc.at[n], tbuf.at[t_slot, n], tsend.at[i, n], tsem.at[t_slot, n], dev(rot4(x, by), y, z, t_core)
                ),
                jnp.logical_and(is1, jnp.logical_not(own)),
            )
    for n in (0, 1):
        pl.when(jnp.logical_and(is1, t_core == 1))(
            lambda: pltpu.make_async_copy(tloc.at[n], tbuf.at[t_slot, n], tsem.at[t_slot, n]).start()
        )

    def piece(i):
        s = (i + 1) // 2
        return rot8(z, jnp.where(lax.rem(i, 2) == 1, -s, s))

    half = pl.ds(pl.multiple_of(k * 128, 128), 128)
    other_half = pl.ds(pl.multiple_of((1 - k) * 128, 128), 128)

    def ring(p, ss, i, z_):
        r = sbuf.at[p, :, half, :]
        return remote(r, r, ss, rsem.at[i], dev(x, y, z_, k))

    def to_sibling(p, i):
        r = sbuf.at[p, :, half, :]
        return remote(r, r, csend.at[i], csem.at[i], dev(x, y, z, 1 - k))

    def arrive(i):
        p = piece(i)
        landed(sbuf.at[p, :, half, :], rsem.at[i])
        odd = lax.rem(i, 2) == 1
        pl.when(jnp.logical_and(odd, i < 7))(lambda: ring(p, rsend.at[i], i + 2, z_up).start())
        pl.when(jnp.logical_and(jnp.logical_not(odd), i < 6))(lambda: ring(p, rsend.at[i], i + 2, z_down).start())
        to_sibling(p, i).start()

    def rows_of(p):
        return pl.ds(pl.multiple_of((2 * lax.rem(p, 4) + p // 4) * B, B), B)

    ups = ((0, 1), (1, -1))

    def relay_copy(i, n, by):
        r = pbuf.at[i, rot4(y, 2), pl.ds(n * 128, 128)]
        return remote(r, relay.at[n, i], esend.at[n, i], esem.at[n, i], dev(x, rot4(y, by), z, k))

    def partial_copy(i, n, by):
        yy = rot4(y, by)
        return remote(
            pbuf.at[i, yy], rbuf.at[n, rows_of(piece(i))], psend.at[n, i], psem.at[n, i], dev(x, yy, z, k)
        )

    def process(i):
        p = piece(i)
        rows = rows_of(p)
        a = [split(sbuf[p, n]) for n in (0, 1)]
        for h in (0, 1):
            acc = mm3(a[0], (th[h, 0], tl[h, 0])) + mm3(a[1], (th[h, 1], tl[h, 1]))
            pbuf[i, 2 * h] = acc[:, :128]
            pbuf[i, 2 * h + 1] = acc[:, 128:]
        for n, by in ups:
            relay_copy(i, n, by).start()
        out[rows, :] = out[rows, :] - pbuf[i, y]

    def pass_on(i):
        for n, by in ups:
            landed(relay.at[n, i], esem.at[n, i])
            yy = rot4(y, by)
            part = pl.ds(n * 128, 128)
            pbuf[i, yy, part] = pbuf[i, yy, part] + relay[n, i]
            partial_copy(i, n, by).start()

    @pl.when(k == 1)
    def _():
        landed(sbuf.at[z], csem.at[0])

    ring(z, rsend.at[0], 1, z_up).start()
    ring(z, rsend.at[8], 2, z_down).start()

    def t_relay(xs, n, by):
        r = tbuf.at[lax.rem(xs, 2), n]
        return remote(r, r, tsend.at[3, 0], tsem.at[lax.rem(xs, 2), n], dev(rot4(x, by), y, z, k))

    for h in (0, 1):
        xs = 2 * k + h
        for n, by in ups:
            landed(tbuf.at[h, n], tsem.at[h, n])
            start(t_relay(xs, n, by), xs == rot4(x, -by))
        for n in (0, 1):
            high, low = split(tbuf[h, n])
            th[h, n] = high
            tl[h, n] = low

    landed(out, lsem.at[1])
    process(0)

    @pl.loop(1, 10)
    def _(i):
        pl.when(i < 8)(lambda: arrive(i))

        @pl.when(jnp.logical_and(i > 1, i < 9))
        def _():
            landed(sbuf.at[piece(i - 1), :, other_half, :], csem.at[i - 1])
            process(i - 1)

        pl.when(i > 1)(lambda: pass_on(i - 2))

    @pl.loop(0, 8)
    def _(i):
        rows = rows_of(piece(i))
        for n in (0, 1):
            landed(rbuf.at[n, rows], psem.at[n, i])
        out[rows, :] = out[rows, :] - (rbuf[0, rows] + rbuf[1, rows])

    for cp, when in sends:
        if when is None:
            cp.wait_send()
        else:
            pl.when(when)(lambda: cp.wait_send())

    @pl.when(k == 0)
    def _():
        remote(sbuf.at[z], sbuf.at[z], csend.at[0], csem.at[0], dev(x, y, z, 1)).wait_send()

    ring(z, rsend.at[0], 1, z_up).wait_send()
    ring(z, rsend.at[8], 2, z_down).wait_send()

    @pl.loop(1, 8)
    def _(i):
        pl.when(i < 6)(lambda: ring(z, rsend.at[i], i + 2, z_up).wait_send())
        to_sibling(z, i).wait_send()

    @pl.loop(0, 8)
    def _(i):
        for n, by in ups:
            relay_copy(i, n, by).wait_send()
            partial_copy(i, n, by).wait_send()


def local(left_panel, upper_inverse, lower_inverse, top_panel, trailing):
    vmem = pl.BlockSpec(memory_space=pltpu.VMEM)
    dma = pltpu.SemaphoreType.DMA
    return pl.pallas_call(
        kernel,
        out_shape=jax.ShapeDtypeStruct(trailing.shape, F32),
        in_specs=[pl.BlockSpec(memory_space=pl.ANY)] * 5,
        out_specs=vmem,
        scratch_shapes=[
            pltpu.VMEM((8, B, B), F32),
            pltpu.VMEM((2048, B), F32),
            pltpu.VMEM((B, 2048), F32),
            pltpu.VMEM((4, 512, B), F32),
            pltpu.VMEM((4, B, 512), F32),
            pltpu.VMEM((8, 2, B, B), F32),
            pltpu.VMEM((2, B, B), F32),
            pltpu.VMEM((2, 2, B, B), F32),
            pltpu.VMEM((2, 2, B, B), BF16),
            pltpu.VMEM((2, 2, B, B), BF16),
            pltpu.VMEM((8, 4, B, 128), F32),
            pltpu.VMEM((2, 2048, 128), F32),
            pltpu.VMEM((2, 8, 128, 128), F32),
            dma((8,)), dma((3,)), dma((2, 3)), dma((4, 4, 2)), dma((4, 6)), dma((2, 2)), dma((4, 2)),
            dma((8,)), dma((9,)), dma((8,)), dma((8,)),
            dma((2, 8)), dma((2, 8)), dma((2, 8)), dma((2, 8)), dma((2,)),
        ],
        compiler_params=pltpu.CompilerParams(
            collective_id=0, has_side_effects=True, vmem_limit_bytes=60 * 2**20
        ),
        name="schur",
    )(left_panel, upper_inverse, lower_inverse, top_panel, trailing)


def solution(mesh):
    placed = (
        P(("row", "col"), "depth"),
        P(None, "depth"),
        P("depth", None),
        P("depth", "col"),
        P("row", ("col", "depth")),
    )
    return jax.shard_map(
        local, mesh=mesh, in_specs=placed, out_specs=P("row", ("col", "depth")), check_vma=False
    )
```

```python
import functools

import jax
import jax.numpy as jnp
from jax import lax
from jax.experimental import pallas as pl
from jax.experimental.pallas import tpu as pltpu
from jax.sharding import PartitionSpec as P

MESH = pl.DeviceIdType.MESH
F32 = jnp.float32
BF16 = jnp.bfloat16
B = 256


def split(v):
    high = v.astype(BF16)
    return high, (v - high.astype(F32)).astype(BF16)


def mm3(a, b):
    (ah, al), (bh, bl) = a, b
    dot = functools.partial(jnp.dot, preferred_element_type=F32)
    return dot(ah, bh) + (dot(ah, bl) + dot(al, bh))


def kernel(
    left, upper, lower, top, trailing, result,
    out, gbuf, uown, lown, ubuf, lbuf, sbuf, tloc, tbuf, th, tl, pbuf, rbuf, relay,
    gsem, xsend, gsend, fsem, fsend, tsem, tsend, rsem, rsend, csem, csend,
    esem, esend, psem, psend, lsem, osem, go,
):
    x = lax.axis_index("row")
    c = lax.axis_index("col")
    d = lax.axis_index("depth")
    k = lax.rem(c, 2)
    zl = c // 2
    y = lax.rem(d, 4)
    zh = d // 4
    z = zh * 4 + zl
    d2 = (1 - zh) * 4 + y

    def dev(x_, y_, z_, k_):
        return (x_, lax.rem(z_, 4) * 2 + k_, (z_ // 4) * 4 + y_)

    def rot4(v, by):
        return lax.rem(v + by + 4, 4)

    def rot8(v, by):
        return lax.rem(v + by + 8, 8)

    def remote(src, dst, ss, rs, device):
        return pltpu.make_async_remote_copy(
            src_ref=src, dst_ref=dst, send_sem=ss, recv_sem=rs, device_id=device, device_id_type=MESH
        )

    def landed(ref, sem):
        pltpu.make_async_copy(ref, ref, sem).wait()

    zo = rot8(z, 4)
    z_up, z_down = rot8(z, 1), rot8(z, -1)
    is0, is1 = k == 0, k == 1

    pl.when(is0)(lambda: pltpu.make_async_copy(upper, uown, lsem.at[0]).start())
    pl.when(is1)(lambda: pltpu.make_async_copy(lower, lown, lsem.at[0]).start())
    pltpu.make_async_copy(trailing, out, lsem.at[1]).start()

    peers = [dev(x, y, z, 1 - k), dev(x, y, zo, 0), dev(x, y, zo, 1), dev(x, y, z_up, k), dev(x, y, z_down, k)]
    peers += [dev(x, rot4(y, i), z, k) for i in (1, 2, 3)]
    peers += [dev(rot4(x, i), y, z, j) for i in (1, 3) for j in (0, 1)]
    barrier = pltpu.get_barrier_semaphore()
    for peer in peers:
        pl.semaphore_signal(barrier, inc=1, device_id=peer, device_id_type=MESH)
    pl.semaphore_wait(barrier, len(peers))

    sends = []

    def start(cp, when=None):
        if when is None:
            cp.start()
        else:
            pl.when(when)(lambda: cp.start())
        sends.append((cp, when))

    is_self = jnp.logical_and(k == 0, zh == 0)
    def send_left(when):
        start(remote(left, gbuf.at[d], xsend.at[0], gsem.at[d], dev(x, y, k * 4 + zl, 0)), when)

    send_left(jnp.logical_and(k == zh, jnp.logical_not(is_self)))
    pl.when(is_self)(lambda: pltpu.make_async_copy(left, gbuf.at[d], gsem.at[d]).start())

    mine = k == x // 2
    for h in (0, 1):
        block = top.at[:, pl.ds(pl.multiple_of(h * 512 + lax.rem(x, 2) * B, B), B)]
        own = jnp.logical_and(k == 1, zh == h)
        start(
            remote(block, gbuf.at[d], xsend.at[1 + h], gsem.at[d], dev(x, y, h * 4 + zl, 1)),
            jnp.logical_and(mine, jnp.logical_not(own)),
        )
        pl.when(jnp.logical_and(mine, own))(
            lambda: pltpu.make_async_copy(block, gbuf.at[d], gsem.at[d]).start()
        )

    edge = jnp.logical_or(zl == 0, zl == 3)
    z_cross = jnp.where(zl == 0, z_down, z_up)
    z_in = jnp.where(zl == 0, z_up, z_down)

    def u_share(g, xs, half=None):
        rows = pl.ds(xs * 128, 128) if half is None else pl.ds(xs * 128 + half * 64, 64)
        return ubuf.at[g, rows]

    def l_share(g, xs, half=None):
        rows = pl.ds(xs * 64, 64) if half is None else pl.ds(xs * 64 + half * 32, 32)
        return lbuf.at[g, rows]

    kinds = ((is0, u_share), (is1, l_share))
    def feed(g, kind):
        uq = upper.at[pl.ds(pl.multiple_of(g * 512 + x * 128, 128), 128), :]
        lq = lower.at[pl.ds(pl.multiple_of(x * 64, 64), 64), pl.ds(g * 512, 512)]
        is_k, share = kinds[kind]
        start(
            remote((uq, lq)[kind], share(g, x), fsend.at[g, 0], fsem.at[g, x, 0], dev(x, y, z_cross, k)),
            jnp.logical_and(jnp.logical_and(edge, is_k), 2 * g <= d),
        )

    def chunk(g):
        wanted = 2 * g <= d2

        @pl.when(wanted)
        def _():
            landed(u_share(g, x), fsem.at[g, x, 0])

        for is_k, share in kinds:
            go = jnp.logical_and(wanted, is_k)
            r = share(g, x)
            start(
                remote(r, r, fsend.at[g, 1], fsem.at[g, x, 0], dev(x, y, z_in, k)), jnp.logical_and(edge, go)
            )
            start(remote(r, r, fsend.at[g, 2], fsem.at[g, x, 0], dev(rot4(x, 1), y, z, k)), go)
            start(remote(r, r, fsend.at[g, 3], fsem.at[g, x, 0], dev(rot4(x, -1), y, z, k)), go)

    def chunk_relay(g):
        wanted = 2 * g <= d2
        for half, by in ((0, 1), (1, -1)):
            xs = rot4(x, -by)

            @pl.when(wanted)
            def _():
                landed(u_share(g, xs), fsem.at[g, xs, 0])

            for is_k, share in kinds:
                r = share(g, xs, half)
                start(
                    remote(r, r, fsend.at[g, 4 + half], fsem.at[g, xs, half], dev(rot4(x, by), y, z, k)),
                    jnp.logical_and(wanted, is_k),
                )

    def gather_y(slot, j):
        for i in (1, 2, 3):
            yy = rot4(y, i)
            start(
                remote(gbuf.at[slot], gbuf.at[slot], gsend.at[j, i - 1], gsem.at[slot], dev(x, yy, z, k)),
                jnp.logical_or(slot < 4, yy > y),
            )

    feed(0, 1)
    feed(1, 1)
    feed(2, 1)
    feed(3, 1)
    landed(gbuf.at[d], gsem.at[d])
    gather_y(d, 0)
    pl.when(is0)(lambda: pl.semaphore_wait(go, 1))
    send_left(jnp.logical_and(is0, zh == 1))
    feed(0, 0)
    feed(1, 0)
    feed(2, 0)
    feed(3, 0)
    chunk(0)
    pl.when(is1)(
        lambda: pl.semaphore_signal(go, inc=1, device_id=dev(x, y, z, 0), device_id_type=MESH)
    )
    send_left(jnp.logical_and(is1, zh == 0))
    chunk(1)
    landed(gbuf.at[d2], gsem.at[d2])
    gather_y(d2, 1)
    chunk_relay(0)
    chunk(2)
    chunk_relay(1)
    chunk(3)
    chunk_relay(2)
    chunk_relay(3)

    landed(uown, lsem.at[0])

    def wait_block(i):
        @pl.when(jnp.logical_and(lax.rem(i, 4) != y, i <= 4 + y))
        def _():
            landed(gbuf.at[i], gsem.at[i])

    def wait_chunk(i):
        g = i // 2
        xs = rot4(x, 2)

        @pl.when(jnp.logical_and(lax.rem(i, 2) == 0, i <= d2))
        def _():
            landed(u_share(g, xs, 0), fsem.at[g, xs, 0])
            landed(u_share(g, xs, 1), fsem.at[g, xs, 1])

    @pl.when(k == 0)
    def _():
        sbuf[z] = jnp.zeros((2, B, B), F32)

        @pl.loop(0, 8)
        def _(i):
            wait_block(i)
            wait_chunk(i)

            @pl.when(i <= d)
            def _():
                f = uown[pl.ds(pl.multiple_of(i * B, B), B), :]
                sbuf[z, zh] += mm3(split(gbuf[i]), split(f))

            @pl.when(i <= d2)
            def _():
                f = ubuf[i // 2, pl.ds(pl.multiple_of(lax.rem(i, 2) * B, B), B), :]
                sbuf[z, 1 - zh] += mm3(split(gbuf[i]), split(f))

        remote(sbuf.at[z], sbuf.at[z], csend.at[0], csem.at[0], dev(x, y, z, 1)).start()

    t_core = x // 2
    t_slot = lax.rem(x, 2)

    @pl.when(k == 1)
    def _():
        tloc[...] = jnp.zeros((2, B, B), F32)

        @pl.loop(0, 8)
        def _(i):
            wait_block(i)
            wait_chunk(i)

            @pl.when(i <= d)
            def _():
                f = lown[:, pl.ds(pl.multiple_of(i * B, B), B)]
                tloc[zh] += mm3(split(f), split(gbuf[i]))

            @pl.when(i <= d2)
            def _():
                f = lbuf[i // 2, :, pl.ds(pl.multiple_of(lax.rem(i, 2) * B, B), B)]
                tloc[1 - zh] += mm3(split(f), split(gbuf[i]))

    for i, by in enumerate((0, 1, -1)):
        own = jnp.logical_and(t_core == 1, i == 0)
        for n in (0, 1):
            start(
                remote(
                    tloc.at[n], tbuf.at[t_slot, n], tsend.at[i, n], tsem.at[t_slot, n], dev(rot4(x, by), y, z, t_core)
                ),
                jnp.logical_and(is1, jnp.logical_not(own)),
            )
    for n in (0, 1):
        pl.when(jnp.logical_and(is1, t_core == 1))(
            lambda: pltpu.make_async_copy(tloc.at[n], tbuf.at[t_slot, n], tsem.at[t_slot, n]).start()
        )

    def piece(i):
        s = (i + 1) // 2
        return rot8(z, jnp.where(lax.rem(i, 2) == 1, -s, s))

    half = pl.ds(pl.multiple_of(k * 128, 128), 128)
    other_half = pl.ds(pl.multiple_of((1 - k) * 128, 128), 128)

    def ring(p, ss, i, z_):
        r = sbuf.at[p, :, half, :]
        return remote(r, r, ss, rsem.at[i], dev(x, y, z_, k))

    def to_sibling(p, i):
        r = sbuf.at[p, :, half, :]
        return remote(r, r, csend.at[i], csem.at[i], dev(x, y, z, 1 - k))

    def arrive(i):
        p = piece(i)
        landed(sbuf.at[p, :, half, :], rsem.at[i])
        odd = lax.rem(i, 2) == 1
        pl.when(jnp.logical_and(odd, i < 7))(lambda: ring(p, rsend.at[i], i + 2, z_up).start())
        pl.when(jnp.logical_and(jnp.logical_not(odd), i < 6))(lambda: ring(p, rsend.at[i], i + 2, z_down).start())
        to_sibling(p, i).start()

    def rows_of(p):
        return pl.ds(pl.multiple_of((2 * lax.rem(p, 4) + p // 4) * B, B), B)

    ups = ((0, 1), (1, -1))

    def relay_copy(i, n, by):
        r = pbuf.at[i, rot4(y, 2), pl.ds(n * 128, 128)]
        return remote(r, relay.at[n, i], esend.at[n, i], esem.at[n, i], dev(x, rot4(y, by), z, k))

    def partial_copy(i, n, by):
        yy = rot4(y, by)
        return remote(
            pbuf.at[i, yy], rbuf.at[n, rows_of(piece(i))], psend.at[n, i], psem.at[n, i], dev(x, yy, z, k)
        )

    def process(i):
        p = piece(i)
        rows = rows_of(p)
        a = [split(sbuf[p, n]) for n in (0, 1)]
        for h in (0, 1):
            acc = mm3(a[0], (th[h, 0], tl[h, 0])) + mm3(a[1], (th[h, 1], tl[h, 1]))
            pbuf[i, 2 * h] = acc[:, :128]
            pbuf[i, 2 * h + 1] = acc[:, 128:]
        for n, by in ups:
            relay_copy(i, n, by).start()
        out[rows, :] = out[rows, :] - pbuf[i, y]

    def pass_on(i):
        for n, by in ups:
            landed(relay.at[n, i], esem.at[n, i])
            yy = rot4(y, by)
            part = pl.ds(n * 128, 128)
            pbuf[i, yy, part] = pbuf[i, yy, part] + relay[n, i]
            partial_copy(i, n, by).start()

    @pl.when(k == 1)
    def _():
        landed(sbuf.at[z], csem.at[0])

    ring(z, rsend.at[0], 1, z_up).start()
    ring(z, rsend.at[8], 2, z_down).start()

    rel = rot4(x, -2 * k)
    t_near = 1 - lax.rem(rel, 2)
    t_half = jnp.where(jnp.logical_or(rel == 0, rel == 3), 1, 0)
    r = tbuf.at[t_near, t_half]
    landed(r, tsem.at[t_near, t_half])
    start(remote(r, r, tsend.at[3, 0], tsem.at[t_near, t_half], dev(rot4(x, 1 - 2 * t_half), y, z, k)))
    for h in (0, 1):
        for n in (0, 1):
            here = jnp.logical_and(t_near == h, t_half == n)
            pl.when(jnp.logical_not(here))(lambda: landed(tbuf.at[h, n], tsem.at[h, n]))
            high, low = split(tbuf[h, n])
            th[h, n] = high
            tl[h, n] = low

    landed(out, lsem.at[1])
    process(0)

    @pl.loop(1, 10)
    def _(i):
        pl.when(i < 8)(lambda: arrive(i))

        @pl.when(jnp.logical_and(i > 1, i < 9))
        def _():
            landed(sbuf.at[piece(i - 1), :, other_half, :], csem.at[i - 1])
            process(i - 1)

        pl.when(i > 1)(lambda: pass_on(i - 2))

    @pl.loop(0, 8)
    def _(i):
        rows = rows_of(piece(i))
        for n in (0, 1):
            landed(rbuf.at[n, rows], psem.at[n, i])
        out[rows, :] = out[rows, :] - (rbuf[0, rows] + rbuf[1, rows])
        pltpu.make_async_copy(out.at[rows], result.at[rows], osem.at[i]).start()

    for cp, when in sends:
        if when is None:
            cp.wait_send()
        else:
            pl.when(when)(lambda: cp.wait_send())

    @pl.when(k == 0)
    def _():
        remote(sbuf.at[z], sbuf.at[z], csend.at[0], csem.at[0], dev(x, y, z, 1)).wait_send()

    ring(z, rsend.at[0], 1, z_up).wait_send()
    ring(z, rsend.at[8], 2, z_down).wait_send()

    @pl.loop(1, 8)
    def _(i):
        pl.when(i < 6)(lambda: ring(z, rsend.at[i], i + 2, z_up).wait_send())
        to_sibling(z, i).wait_send()

    @pl.loop(0, 8)
    def _(i):
        for n, by in ups:
            relay_copy(i, n, by).wait_send()
            partial_copy(i, n, by).wait_send()
        rows = rows_of(piece(i))
        pltpu.make_async_copy(out.at[rows], result.at[rows], osem.at[i]).wait()


def local(left_panel, upper_inverse, lower_inverse, top_panel, trailing):
    dma = pltpu.SemaphoreType.DMA
    return pl.pallas_call(
        kernel,
        out_shape=jax.ShapeDtypeStruct(trailing.shape, F32),
        in_specs=[pl.BlockSpec(memory_space=pl.ANY)] * 5,
        out_specs=pl.BlockSpec(memory_space=pl.ANY),
        scratch_shapes=[
            pltpu.VMEM((2048, 128), F32),
            pltpu.VMEM((8, B, B), F32),
            pltpu.VMEM((2048, B), F32),
            pltpu.VMEM((B, 2048), F32),
            pltpu.VMEM((4, 512, B), F32),
            pltpu.VMEM((4, B, 512), F32),
            pltpu.VMEM((8, 2, B, B), F32),
            pltpu.VMEM((2, B, B), F32),
            pltpu.VMEM((2, 2, B, B), F32),
            pltpu.VMEM((2, 2, B, B), BF16),
            pltpu.VMEM((2, 2, B, B), BF16),
            pltpu.VMEM((8, 4, B, 128), F32),
            pltpu.VMEM((2, 2048, 128), F32),
            pltpu.VMEM((2, 8, 128, 128), F32),
            dma((8,)), dma((3,)), dma((2, 3)), dma((4, 4, 2)), dma((4, 6)), dma((2, 2)), dma((4, 2)),
            dma((8,)), dma((9,)), dma((8,)), dma((8,)),
            dma((2, 8)), dma((2, 8)), dma((2, 8)), dma((2, 8)), dma((2,)), dma((8,)), pltpu.SemaphoreType.REGULAR,
        ],
        compiler_params=pltpu.CompilerParams(
            collective_id=0, has_side_effects=True, vmem_limit_bytes=60 * 2**20
        ),
        name="schur",
    )(left_panel, upper_inverse, lower_inverse, top_panel, trailing)


def solution(mesh):
    placed = (
        P(("row", "col"), "depth"),
        P(None, "depth"),
        P("depth", None),
        P("depth", "col"),
        P("row", ("col", "depth")),
    )
    return jax.shard_map(
        local, mesh=mesh, in_specs=placed, out_specs=P("row", ("col", "depth")), check_vma=False
    )
```

```python
import functools

import jax
import jax.numpy as jnp
from jax import lax
from jax.experimental import pallas as pl
from jax.experimental.pallas import tpu as pltpu
from jax.sharding import PartitionSpec as P

MESH = pl.DeviceIdType.MESH
F32 = jnp.float32
BF16 = jnp.bfloat16
B = 256


def split(v):
    high = v.astype(BF16)
    return high, (v - high.astype(F32)).astype(BF16)


def mm3(a, b):
    (ah, al), (bh, bl) = a, b
    dot = functools.partial(jnp.dot, preferred_element_type=F32)
    return dot(ah, bh) + (dot(ah, bl) + dot(al, bh))


def kernel(
    left, upper, lower, top, trailing, result,
    out, gbuf, uown, lown, ubuf, lbuf, sbuf, tloc, tbuf, th, tl, pbuf, rbuf, relay,
    gsem, xsend, gsend, fsem, fsend, tsem, tsend, rsem, rsend, csem, csend,
    esem, esend, psem, psend, lsem, osem, go,
):
    x = lax.axis_index("row")
    c = lax.axis_index("col")
    d = lax.axis_index("depth")
    k = lax.rem(c, 2)
    zl = c // 2
    y = lax.rem(d, 4)
    zh = d // 4
    z = zh * 4 + zl
    d2 = (1 - zh) * 4 + y

    def dev(x_, y_, z_, k_):
        return (x_, lax.rem(z_, 4) * 2 + k_, (z_ // 4) * 4 + y_)

    def rot4(v, by):
        return lax.rem(v + by + 4, 4)

    def rot8(v, by):
        return lax.rem(v + by + 8, 8)

    def remote(src, dst, ss, rs, device):
        return pltpu.make_async_remote_copy(
            src_ref=src, dst_ref=dst, send_sem=ss, recv_sem=rs, device_id=device, device_id_type=MESH
        )

    def landed(ref, sem):
        pltpu.make_async_copy(ref, ref, sem).wait()

    zo = rot8(z, 4)
    z_up, z_down = rot8(z, 1), rot8(z, -1)
    is0, is1 = k == 0, k == 1

    pl.when(is0)(lambda: pltpu.make_async_copy(upper, uown, lsem.at[0]).start())
    pl.when(is1)(lambda: pltpu.make_async_copy(lower, lown, lsem.at[0]).start())
    pltpu.make_async_copy(trailing, out, lsem.at[1]).start()

    peers = [dev(x, y, z, 1 - k), dev(x, y, zo, 0), dev(x, y, zo, 1), dev(x, y, z_up, k), dev(x, y, z_down, k)]
    peers += [dev(x, rot4(y, i), z, k) for i in (1, 2, 3)]
    peers += [dev(rot4(x, i), y, z, j) for i in (1, 3) for j in (0, 1)]
    barrier = pltpu.get_barrier_semaphore()
    for peer in peers:
        pl.semaphore_signal(barrier, inc=1, device_id=peer, device_id_type=MESH)
    pl.semaphore_wait(barrier, len(peers))

    sends = []

    def start(cp, when=None):
        if when is None:
            cp.start()
        else:
            pl.when(when)(lambda: cp.start())
        sends.append((cp, when))

    is_self = jnp.logical_and(k == 0, zh == 0)
    def send_left(when):
        start(remote(left, gbuf.at[d], xsend.at[0], gsem.at[d], dev(x, y, k * 4 + zl, 0)), when)

    send_left(jnp.logical_and(k == zh, jnp.logical_not(is_self)))
    pl.when(is_self)(lambda: pltpu.make_async_copy(left, gbuf.at[d], gsem.at[d]).start())

    mine = k == x // 2
    for h in (0, 1):
        block = top.at[:, pl.ds(pl.multiple_of(h * 512 + lax.rem(x, 2) * B, B), B)]
        own = jnp.logical_and(k == 1, zh == h)
        start(
            remote(block, gbuf.at[d], xsend.at[1 + h], gsem.at[d], dev(x, y, h * 4 + zl, 1)),
            jnp.logical_and(mine, jnp.logical_not(own)),
        )
        pl.when(jnp.logical_and(mine, own))(
            lambda: pltpu.make_async_copy(block, gbuf.at[d], gsem.at[d]).start()
        )

    edge = jnp.logical_or(zl == 0, zl == 3)
    z_cross = jnp.where(zl == 0, z_down, z_up)
    z_in = jnp.where(zl == 0, z_up, z_down)

    def u_share(g, xs, half=None):
        rows = pl.ds(xs * 128, 128) if half is None else pl.ds(xs * 128 + half * 64, 64)
        return ubuf.at[g, rows]

    def l_share(g, xs, half=None):
        rows = pl.ds(xs * 64, 64) if half is None else pl.ds(xs * 64 + half * 32, 32)
        return lbuf.at[g, rows]

    kinds = ((is0, u_share), (is1, l_share))
    def feed(g, kind):
        uq = upper.at[pl.ds(pl.multiple_of(g * 512 + x * 128, 128), 128), :]
        lq = lower.at[pl.ds(pl.multiple_of(x * 64, 64), 64), pl.ds(g * 512, 512)]
        is_k, share = kinds[kind]
        start(
            remote((uq, lq)[kind], share(g, x), fsend.at[g, 0], fsem.at[g, x, 0], dev(x, y, z_cross, k)),
            jnp.logical_and(jnp.logical_and(edge, is_k), 2 * g <= d),
        )

    def chunk(g):
        wanted = 2 * g <= d2

        @pl.when(wanted)
        def _():
            landed(u_share(g, x), fsem.at[g, x, 0])

        for is_k, share in kinds:
            go = jnp.logical_and(wanted, is_k)
            r = share(g, x)
            start(
                remote(r, r, fsend.at[g, 1], fsem.at[g, x, 0], dev(x, y, z_in, k)), jnp.logical_and(edge, go)
            )
            start(remote(r, r, fsend.at[g, 2], fsem.at[g, x, 0], dev(rot4(x, 1), y, z, k)), go)
            start(remote(r, r, fsend.at[g, 3], fsem.at[g, x, 0], dev(rot4(x, -1), y, z, k)), go)

    def chunk_relay(g):
        wanted = 2 * g <= d2
        for half, by in ((0, 1), (1, -1)):
            xs = rot4(x, -by)

            @pl.when(wanted)
            def _():
                landed(u_share(g, xs), fsem.at[g, xs, 0])

            for is_k, share in kinds:
                r = share(g, xs, half)
                start(
                    remote(r, r, fsend.at[g, 4 + half], fsem.at[g, xs, half], dev(rot4(x, by), y, z, k)),
                    jnp.logical_and(wanted, is_k),
                )

    def gather_y(slot, j):
        for i in (1, 2, 3):
            yy = rot4(y, i)
            start(
                remote(gbuf.at[slot], gbuf.at[slot], gsend.at[j, i - 1], gsem.at[slot], dev(x, yy, z, k)),
                jnp.logical_or(slot < 4, yy > y),
            )

    feed(0, 1)
    feed(1, 1)
    feed(2, 1)
    feed(3, 1)
    landed(gbuf.at[d], gsem.at[d])
    gather_y(d, 0)
    pl.when(is0)(lambda: pl.semaphore_wait(go, 1))
    send_left(jnp.logical_and(is0, zh == 1))
    feed(0, 0)
    feed(1, 0)
    feed(2, 0)
    feed(3, 0)
    chunk(0)
    pl.when(is1)(
        lambda: pl.semaphore_signal(go, inc=1, device_id=dev(x, y, z, 0), device_id_type=MESH)
    )
    send_left(jnp.logical_and(is1, zh == 0))
    chunk(1)
    landed(gbuf.at[d2], gsem.at[d2])
    gather_y(d2, 1)
    chunk_relay(0)
    chunk(2)
    chunk_relay(1)
    chunk(3)
    chunk_relay(2)
    chunk_relay(3)

    landed(uown, lsem.at[0])

    def wait_block(i):
        @pl.when(jnp.logical_and(lax.rem(i, 4) != y, i <= 4 + y))
        def _():
            landed(gbuf.at[i], gsem.at[i])

    def wait_chunk(i):
        g = i // 2
        xs = rot4(x, 2)

        @pl.when(jnp.logical_and(lax.rem(i, 2) == 0, i <= d2))
        def _():
            landed(u_share(g, xs, 0), fsem.at[g, xs, 0])
            landed(u_share(g, xs, 1), fsem.at[g, xs, 1])

    @pl.when(k == 0)
    def _():
        sbuf[z] = jnp.zeros((2, B, B), F32)

        @pl.loop(0, 8)
        def _(i):
            wait_block(i)

            @pl.when(i <= d)
            def _():
                f = uown[pl.ds(pl.multiple_of(i * B, B), B), :]
                sbuf[z, zh] += mm3(split(gbuf[i]), split(f))

        @pl.loop(0, 8)
        def _(i):
            wait_chunk(i)

            @pl.when(i <= d2)
            def _():
                f = ubuf[i // 2, pl.ds(pl.multiple_of(lax.rem(i, 2) * B, B), B), :]
                sbuf[z, 1 - zh] += mm3(split(gbuf[i]), split(f))

        remote(sbuf.at[z], sbuf.at[z], csend.at[0, 0], csem.at[0, 0], dev(x, y, z, 1)).start()

    t_core = x // 2
    t_slot = lax.rem(x, 2)

    @pl.when(k == 1)
    def _():
        tloc[...] = jnp.zeros((2, B, B), F32)

        @pl.loop(0, 8)
        def _(i):
            wait_block(i)

            @pl.when(i <= d)
            def _():
                f = lown[:, pl.ds(pl.multiple_of(i * B, B), B)]
                tloc[zh] += mm3(split(f), split(gbuf[i]))

        @pl.loop(0, 8)
        def _(i):
            wait_chunk(i)

            @pl.when(i <= d2)
            def _():
                f = lbuf[i // 2, :, pl.ds(pl.multiple_of(lax.rem(i, 2) * B, B), B)]
                tloc[1 - zh] += mm3(split(f), split(gbuf[i]))

    for i, by in enumerate((0, 1, -1)):
        own = jnp.logical_and(t_core == 1, i == 0)
        for n in (0, 1):
            start(
                remote(
                    tloc.at[n], tbuf.at[t_slot, n], tsend.at[i, n], tsem.at[t_slot, n], dev(rot4(x, by), y, z, t_core)
                ),
                jnp.logical_and(is1, jnp.logical_not(own)),
            )
    for n in (0, 1):
        pl.when(jnp.logical_and(is1, t_core == 1))(
            lambda: pltpu.make_async_copy(tloc.at[n], tbuf.at[t_slot, n], tsem.at[t_slot, n]).start()
        )

    def piece(i):
        s = (i + 1) // 2
        return rot8(z, jnp.where(lax.rem(i, 2) == 1, -s, s))

    def quarter(p, core, q):
        return sbuf.at[p, :, pl.ds(pl.multiple_of(core * 128 + q * 64, 64), 64), :]

    def ring(p, ss, i, q, z_):
        r = quarter(p, k, q)
        return remote(r, r, ss, rsem.at[i, q], dev(x, y, z_, k))

    def to_sibling(p, i, q):
        r = quarter(p, k, q)
        return remote(r, r, csend.at[i, q], csem.at[i, q], dev(x, y, z, 1 - k))

    def ring_on(p, i, q):
        odd = lax.rem(i, 2) == 1
        go = jnp.where(odd, i < 7 - 2 * q, i < 5 + 2 * q)
        return ring(p, rsend.at[i, q], jnp.minimum(i + 2, 7), q, jnp.where(odd, z_up, z_down)), go

    def arrive(i):
        p = piece(i)
        for q in (0, 1):
            landed(quarter(p, k, q), rsem.at[i, q])
            cp, go = ring_on(p, i, q)
            pl.when(go)(lambda: cp.start())
            to_sibling(p, i, q).start()

    def whole(i):
        for q in (0, 1):
            landed(quarter(piece(i), 1 - k, q), csem.at[i, q])

    def rows_of(p):
        return pl.ds(pl.multiple_of((2 * lax.rem(p, 4) + p // 4) * B, B), B)

    ups = ((0, 1), (1, -1))

    def relay_copy(i, n, by):
        r = pbuf.at[i, rot4(y, 2), pl.ds(n * 128, 128)]
        return remote(r, relay.at[n, i], esend.at[n, i], esem.at[n, i], dev(x, rot4(y, by), z, k))

    def partial_copy(i, n, by, m):
        yy = rot4(y, by)
        rows = pl.ds(pl.multiple_of(rows_of(piece(i)).start + m * 128, 128), 128)
        return remote(
            pbuf.at[i, yy, pl.ds(m * 128, 128)], rbuf.at[n, rows], psend.at[n, m, i], psem.at[n, m, i],
            dev(x, yy, z, k),
        )

    def process(i):
        p = piece(i)
        rows = rows_of(p)
        a = [split(sbuf[p, n]) for n in (0, 1)]
        for h in (0, 1):
            acc = mm3(a[0], (th[h, 0], tl[h, 0])) + mm3(a[1], (th[h, 1], tl[h, 1]))
            pbuf[i, 2 * h] = acc[:, :128]
            pbuf[i, 2 * h + 1] = acc[:, 128:]
        for n, by in ups:
            relay_copy(i, n, by).start()
            partial_copy(i, n, by, 1 - n).start()
        out[rows, :] = out[rows, :] - pbuf[i, y]

    def pass_on(i):
        for n, by in ups:
            landed(relay.at[n, i], esem.at[n, i])
            yy = rot4(y, by)
            part = pl.ds(n * 128, 128)
            pbuf[i, yy, part] = pbuf[i, yy, part] + relay[n, i]
            partial_copy(i, n, by, n).start()

    @pl.when(k == 1)
    def _():
        landed(sbuf.at[z], csem.at[0, 0])

    for q in (0, 1):
        ring(z, rsend.at[0, q], 1, q, z_up).start()
        ring(z, rsend.at[8, q], 2, q, z_down).start()

    rel = rot4(x, -2 * k)
    t_near = 1 - lax.rem(rel, 2)
    t_half = jnp.where(jnp.logical_or(rel == 0, rel == 3), 1, 0)
    r = tbuf.at[t_near, t_half]
    landed(r, tsem.at[t_near, t_half])
    start(remote(r, r, tsend.at[3, 0], tsem.at[t_near, t_half], dev(rot4(x, 1 - 2 * t_half), y, z, k)))
    for h in (0, 1):
        for n in (0, 1):
            here = jnp.logical_and(t_near == h, t_half == n)
            pl.when(jnp.logical_not(here))(lambda: landed(tbuf.at[h, n], tsem.at[h, n]))
            high, low = split(tbuf[h, n])
            th[h, n] = high
            tl[h, n] = low

    landed(out, lsem.at[1])
    process(0)

    arrive(1)

    @pl.loop(1, 9)
    def _(i):
        @pl.when(i < 8)
        def _():
            whole(i)
            process(i)

        pl.when(i < 7)(lambda: arrive(i + 1))
        pass_on(i - 1)

    @pl.loop(0, 8)
    def _(i):
        rows = rows_of(piece(i))
        for n in (0, 1):
            for m in (0, 1):
                landed(rbuf.at[n, pl.ds(pl.multiple_of(rows.start + m * 128, 128), 128)], psem.at[n, m, i])
        out[rows, :] = out[rows, :] - (rbuf[0, rows] + rbuf[1, rows])
        pltpu.make_async_copy(out.at[rows], result.at[rows], osem.at[i]).start()

    for cp, when in sends:
        if when is None:
            cp.wait_send()
        else:
            pl.when(when)(lambda: cp.wait_send())

    @pl.when(k == 0)
    def _():
        remote(sbuf.at[z], sbuf.at[z], csend.at[0, 0], csem.at[0, 0], dev(x, y, z, 1)).wait_send()

    for q in (0, 1):
        ring(z, rsend.at[0, q], 1, q, z_up).wait_send()
        ring(z, rsend.at[8, q], 2, q, z_down).wait_send()

    @pl.loop(1, 8)
    def _(i):
        for q in (0, 1):
            cp, go = ring_on(z, i, q)
            pl.when(go)(lambda: cp.wait_send())
            to_sibling(z, i, q).wait_send()

    @pl.loop(0, 8)
    def _(i):
        for n, by in ups:
            relay_copy(i, n, by).wait_send()
            for m in (0, 1):
                partial_copy(i, n, by, m).wait_send()
        rows = rows_of(piece(i))
        pltpu.make_async_copy(out.at[rows], result.at[rows], osem.at[i]).wait()


def local(left_panel, upper_inverse, lower_inverse, top_panel, trailing):
    dma = pltpu.SemaphoreType.DMA
    return pl.pallas_call(
        kernel,
        out_shape=jax.ShapeDtypeStruct(trailing.shape, F32),
        in_specs=[pl.BlockSpec(memory_space=pl.ANY)] * 5,
        out_specs=pl.BlockSpec(memory_space=pl.ANY),
        scratch_shapes=[
            pltpu.VMEM((2048, 128), F32),
            pltpu.VMEM((8, B, B), F32),
            pltpu.VMEM((2048, B), F32),
            pltpu.VMEM((B, 2048), F32),
            pltpu.VMEM((4, 512, B), F32),
            pltpu.VMEM((4, B, 512), F32),
            pltpu.VMEM((8, 2, B, B), F32),
            pltpu.VMEM((2, B, B), F32),
            pltpu.VMEM((2, 2, B, B), F32),
            pltpu.VMEM((2, 2, B, B), BF16),
            pltpu.VMEM((2, 2, B, B), BF16),
            pltpu.VMEM((8, 4, B, 128), F32),
            pltpu.VMEM((2, 2048, 128), F32),
            pltpu.VMEM((2, 8, 128, 128), F32),
            dma((8,)), dma((3,)), dma((2, 3)), dma((4, 4, 2)), dma((4, 6)), dma((2, 2)), dma((4, 2)),
            dma((8, 2)), dma((9, 2)), dma((8, 2)), dma((8, 2)),
            dma((2, 8)), dma((2, 8)), dma((2, 2, 8)), dma((2, 2, 8)), dma((2,)), dma((8,)), pltpu.SemaphoreType.REGULAR,
        ],
        compiler_params=pltpu.CompilerParams(
            collective_id=0, has_side_effects=True, vmem_limit_bytes=60 * 2**20
        ),
        name="schur",
    )(left_panel, upper_inverse, lower_inverse, top_panel, trailing)


def solution(mesh):
    placed = (
        P(("row", "col"), "depth"),
        P(None, "depth"),
        P("depth", None),
        P("depth", "col"),
        P("row", ("col", "depth")),
    )
    return jax.shard_map(
        local, mesh=mesh, in_specs=placed, out_specs=P("row", ("col", "depth")), check_vma=False
    )
```

```python
import functools

import jax
import jax.numpy as jnp
from jax import lax
from jax.experimental import pallas as pl
from jax.experimental.pallas import tpu as pltpu
from jax.sharding import PartitionSpec as P

MESH = pl.DeviceIdType.MESH
F32 = jnp.float32
BF16 = jnp.bfloat16
B = 256


def split(v):
    high = v.astype(BF16)
    return high, (v - high.astype(F32)).astype(BF16)


def mm3(a, b):
    (ah, al), (bh, bl) = a, b
    dot = functools.partial(jnp.dot, preferred_element_type=F32)
    return dot(ah, bh) + (dot(ah, bl) + dot(al, bh))


def kernel(
    left, upper, lower, top, trailing, result,
    out, gbuf, uown, lown, ubuf, lbuf, sbuf, tloc, tbuf, th, tl, pbuf, rbuf, relay,
    gsem, xsend, gsend, fsem, fsend, tsem, tsend, rsem, rsend, csem, csend,
    esem, esend, psem, psend, lsem, osem, go,
):
    x = lax.axis_index("row")
    c = lax.axis_index("col")
    d = lax.axis_index("depth")
    k = lax.rem(c, 2)
    zl = c // 2
    y = lax.rem(d, 4)
    zh = d // 4
    z = zh * 4 + zl
    d2 = (1 - zh) * 4 + y

    def dev(x_, y_, z_, k_):
        return (x_, lax.rem(z_, 4) * 2 + k_, (z_ // 4) * 4 + y_)

    def rot4(v, by):
        return lax.rem(v + by + 4, 4)

    def rot8(v, by):
        return lax.rem(v + by + 8, 8)

    def remote(src, dst, ss, rs, device):
        return pltpu.make_async_remote_copy(
            src_ref=src, dst_ref=dst, send_sem=ss, recv_sem=rs, device_id=device, device_id_type=MESH
        )

    def landed(ref, sem):
        pltpu.make_async_copy(ref, ref, sem).wait()

    zo = rot8(z, 4)
    z_up, z_down = rot8(z, 1), rot8(z, -1)
    is0, is1 = k == 0, k == 1

    pl.when(is0)(lambda: pltpu.make_async_copy(upper, uown, lsem.at[0]).start())
    pl.when(is1)(lambda: pltpu.make_async_copy(lower, lown, lsem.at[0]).start())
    pltpu.make_async_copy(trailing, out, lsem.at[1]).start()

    peers = [dev(x, y, z, 1 - k), dev(x, y, zo, 0), dev(x, y, zo, 1), dev(x, y, z_up, k), dev(x, y, z_down, k)]
    peers += [dev(x, rot4(y, i), z, k) for i in (1, 2, 3)]
    peers += [dev(rot4(x, i), y, z, j) for i in (1, 3) for j in (0, 1)]
    barrier = pltpu.get_barrier_semaphore()
    for peer in peers:
        pl.semaphore_signal(barrier, inc=1, device_id=peer, device_id_type=MESH)
    pl.semaphore_wait(barrier, len(peers))

    sends = []

    def start(cp, when=None):
        if when is None:
            cp.start()
        else:
            pl.when(when)(lambda: cp.start())
        sends.append((cp, when))

    is_self = jnp.logical_and(k == 0, zh == 0)
    def send_left(when):
        start(remote(left, gbuf.at[d], xsend.at[0], gsem.at[d], dev(x, y, k * 4 + zl, 0)), when)

    send_left(jnp.logical_and(k == zh, jnp.logical_not(is_self)))
    pl.when(is_self)(lambda: pltpu.make_async_copy(left, gbuf.at[d], gsem.at[d]).start())

    mine = k == x // 2
    for h in (0, 1):
        block = top.at[:, pl.ds(pl.multiple_of(h * 512 + lax.rem(x, 2) * B, B), B)]
        own = jnp.logical_and(k == 1, zh == h)
        start(
            remote(block, gbuf.at[d], xsend.at[1 + h], gsem.at[d], dev(x, y, h * 4 + zl, 1)),
            jnp.logical_and(mine, jnp.logical_not(own)),
        )
        pl.when(jnp.logical_and(mine, own))(
            lambda: pltpu.make_async_copy(block, gbuf.at[d], gsem.at[d]).start()
        )

    edge = jnp.logical_or(zl == 0, zl == 3)
    z_cross = jnp.where(zl == 0, z_down, z_up)
    z_in = jnp.where(zl == 0, z_up, z_down)

    def u_share(g, xs, half=None):
        rows = pl.ds(xs * 128, 128) if half is None else pl.ds(xs * 128 + half * 64, 64)
        return ubuf.at[g, rows]

    def l_share(g, xs, half=None):
        rows = pl.ds(xs * 64, 64) if half is None else pl.ds(xs * 64 + half * 32, 32)
        return lbuf.at[g, rows]

    kinds = ((is0, u_share), (is1, l_share))
    def feed(g, kind):
        uq = upper.at[pl.ds(pl.multiple_of(g * 512 + x * 128, 128), 128), :]
        lq = lower.at[pl.ds(pl.multiple_of(x * 64, 64), 64), pl.ds(g * 512, 512)]
        is_k, share = kinds[kind]
        start(
            remote((uq, lq)[kind], share(g, x), fsend.at[g, 0], fsem.at[g, x, 0], dev(x, y, z_cross, k)),
            jnp.logical_and(jnp.logical_and(edge, is_k), 2 * g <= d),
        )

    def chunk(g):
        wanted = 2 * g <= d2

        @pl.when(wanted)
        def _():
            landed(u_share(g, x), fsem.at[g, x, 0])

        for is_k, share in kinds:
            go = jnp.logical_and(wanted, is_k)
            r = share(g, x)
            start(
                remote(r, r, fsend.at[g, 1], fsem.at[g, x, 0], dev(x, y, z_in, k)), jnp.logical_and(edge, go)
            )
            start(remote(r, r, fsend.at[g, 2], fsem.at[g, x, 0], dev(rot4(x, 1), y, z, k)), go)
            start(remote(r, r, fsend.at[g, 3], fsem.at[g, x, 0], dev(rot4(x, -1), y, z, k)), go)

    def chunk_relay(g):
        wanted = 2 * g <= d2
        for half, by in ((0, 1), (1, -1)):
            xs = rot4(x, -by)

            @pl.when(wanted)
            def _():
                landed(u_share(g, xs), fsem.at[g, xs, 0])

            for is_k, share in kinds:
                r = share(g, xs, half)
                start(
                    remote(r, r, fsend.at[g, 4 + half], fsem.at[g, xs, half], dev(rot4(x, by), y, z, k)),
                    jnp.logical_and(wanted, is_k),
                )

    def gather_y(slot, j):
        for i in (1, 2, 3):
            yy = rot4(y, i)
            start(
                remote(gbuf.at[slot], gbuf.at[slot], gsend.at[j, i - 1], gsem.at[slot], dev(x, yy, z, k)),
                jnp.logical_or(slot < 4, yy > y),
            )

    feed(0, 1)
    feed(1, 1)
    feed(2, 1)
    feed(3, 1)
    landed(gbuf.at[d], gsem.at[d])
    gather_y(d, 0)
    pl.when(is0)(lambda: pl.semaphore_wait(go, 1))
    send_left(jnp.logical_and(is0, zh == 1))
    feed(0, 0)
    feed(1, 0)
    feed(2, 0)
    feed(3, 0)
    chunk(0)
    pl.when(is1)(
        lambda: pl.semaphore_signal(go, inc=1, device_id=dev(x, y, z, 0), device_id_type=MESH)
    )
    send_left(jnp.logical_and(is1, zh == 0))
    chunk(1)
    chunk_relay(0)
    chunk(2)
    landed(gbuf.at[d2], gsem.at[d2])
    gather_y(d2, 1)
    chunk_relay(1)
    chunk(3)
    chunk_relay(2)
    chunk_relay(3)

    landed(uown, lsem.at[0])

    def wait_block(i):
        @pl.when(jnp.logical_and(lax.rem(i, 4) != y, i <= 4 + y))
        def _():
            landed(gbuf.at[i], gsem.at[i])

    def wait_chunk(i):
        g = i // 2
        xs = rot4(x, 2)

        @pl.when(jnp.logical_and(lax.rem(i, 2) == 0, i <= d2))
        def _():
            landed(u_share(g, xs, 0), fsem.at[g, xs, 0])
            landed(u_share(g, xs, 1), fsem.at[g, xs, 1])

    @pl.when(k == 0)
    def _():
        sbuf[z] = jnp.zeros((2, B, B), F32)

        @pl.loop(0, 8)
        def _(i):
            wait_block(i)

            @pl.when(i <= d)
            def _():
                f = uown[pl.ds(pl.multiple_of(i * B, B), B), :]
                sbuf[z, zh] += mm3(split(gbuf[i]), split(f))

        @pl.loop(0, 8)
        def _(i):
            wait_chunk(i)

            @pl.when(i <= d2)
            def _():
                f = ubuf[i // 2, pl.ds(pl.multiple_of(lax.rem(i, 2) * B, B), B), :]
                sbuf[z, 1 - zh] += mm3(split(gbuf[i]), split(f))

        remote(sbuf.at[z], sbuf.at[z], csend.at[0, 0], csem.at[0, 0], dev(x, y, z, 1)).start()

    t_core = x // 2
    t_slot = lax.rem(x, 2)

    @pl.when(k == 1)
    def _():
        tloc[...] = jnp.zeros((2, B, B), F32)

        @pl.loop(0, 8)
        def _(i):
            wait_block(i)

            @pl.when(i <= d)
            def _():
                f = lown[:, pl.ds(pl.multiple_of(i * B, B), B)]
                tloc[zh] += mm3(split(f), split(gbuf[i]))

        @pl.loop(0, 8)
        def _(i):
            wait_chunk(i)

            @pl.when(i <= d2)
            def _():
                f = lbuf[i // 2, :, pl.ds(pl.multiple_of(lax.rem(i, 2) * B, B), B)]
                tloc[1 - zh] += mm3(split(f), split(gbuf[i]))

    for i, by in enumerate((0, 1, -1)):
        own = jnp.logical_and(t_core == 1, i == 0)
        for n in (0, 1):
            start(
                remote(
                    tloc.at[n], tbuf.at[t_slot, n], tsend.at[i, n], tsem.at[t_slot, n], dev(rot4(x, by), y, z, t_core)
                ),
                jnp.logical_and(is1, jnp.logical_not(own)),
            )
    for n in (0, 1):
        pl.when(jnp.logical_and(is1, t_core == 1))(
            lambda: pltpu.make_async_copy(tloc.at[n], tbuf.at[t_slot, n], tsem.at[t_slot, n]).start()
        )

    rel = rot4(x, -2 * k)
    t_near = 1 - lax.rem(rel, 2)
    t_half = jnp.where(jnp.logical_or(rel == 0, rel == 3), 1, 0)
    r = tbuf.at[t_near, t_half]
    pass_t = remote(r, r, tsend.at[3, 0], tsem.at[t_near, t_half], dev(rot4(x, 1 - 2 * t_half), y, z, k))
    pl.when(is1)(lambda: landed(r, tsem.at[t_near, t_half]))
    start(pass_t, is1)

    def piece(i):
        s = (i + 1) // 2
        return rot8(z, jnp.where(lax.rem(i, 2) == 1, -s, s))

    def quarter(p, core, q):
        return sbuf.at[p, :, pl.ds(pl.multiple_of(core * 128 + q * 64, 64), 64), :]

    def ring(p, ss, i, q, z_):
        r = quarter(p, k, q)
        return remote(r, r, ss, rsem.at[i, q], dev(x, y, z_, k))

    def to_sibling(p, i, q):
        r = quarter(p, k, q)
        return remote(r, r, csend.at[i, q], csem.at[i, q], dev(x, y, z, 1 - k))

    def ring_on(p, i, q):
        odd = lax.rem(i, 2) == 1
        go = jnp.where(odd, i < 7 - 2 * q, i < 5 + 2 * q)
        return ring(p, rsend.at[i, q], jnp.minimum(i + 2, 7), q, jnp.where(odd, z_up, z_down)), go

    def arrive(i):
        p = piece(i)
        for q in (0, 1):
            landed(quarter(p, k, q), rsem.at[i, q])
            cp, go = ring_on(p, i, q)
            pl.when(go)(lambda: cp.start())
            to_sibling(p, i, q).start()

    def whole(i):
        for q in (0, 1):
            landed(quarter(piece(i), 1 - k, q), csem.at[i, q])

    def rows_of(p):
        return pl.ds(pl.multiple_of((2 * lax.rem(p, 4) + p // 4) * B, B), B)

    ups = ((0, 1), (1, -1))

    def relay_copy(i, n, by):
        r = pbuf.at[i, rot4(y, 2), pl.ds(n * 128, 128)]
        return remote(r, relay.at[n, i], esend.at[n, i], esem.at[n, i], dev(x, rot4(y, by), z, k))

    def partial_copy(i, n, by, m):
        yy = rot4(y, by)
        rows = pl.ds(pl.multiple_of(rows_of(piece(i)).start + m * 128, 128), 128)
        return remote(
            pbuf.at[i, yy, pl.ds(m * 128, 128)], rbuf.at[n, rows], psend.at[n, m, i], psem.at[n, m, i],
            dev(x, yy, z, k),
        )

    def process(i):
        rows = rows_of(piece(i))
        p = piece(i)
        a = split(jnp.concatenate([sbuf[p, 0], sbuf[p, 1]], axis=1))
        for n_h, h in enumerate((1 - y // 2, y // 2)):
            acc = mm3(a, (th[h].reshape(2 * B, B), tl[h].reshape(2 * B, B)))
            pbuf[i, 2 * h] = acc[:, :128]
            pbuf[i, 2 * h + 1] = acc[:, 128:]
            if n_h == 0:
                for n, by in ups:
                    relay_copy(i, n, by).start()
        for n, by in ups:
            partial_copy(i, n, by, 1 - n).start()
        out[rows, :] = out[rows, :] - pbuf[i, y]

    def pass_on(i):
        for n, by in ups:
            landed(relay.at[n, i], esem.at[n, i])
            yy = rot4(y, by)
            part = pl.ds(n * 128, 128)
            pbuf[i, yy, part] = pbuf[i, yy, part] + relay[n, i]
            partial_copy(i, n, by, n).start()

    @pl.when(k == 1)
    def _():
        landed(sbuf.at[z], csem.at[0, 0])

    for q in (0, 1):
        ring(z, rsend.at[0, q], 1, q, z_up).start()
        ring(z, rsend.at[8, q], 2, q, z_down).start()

    pl.when(is0)(lambda: landed(r, tsem.at[t_near, t_half]))
    start(pass_t, is0)
    for h in (0, 1):
        for n in (0, 1):
            here = jnp.logical_and(t_near == h, t_half == n)
            pl.when(jnp.logical_not(here))(lambda: landed(tbuf.at[h, n], tsem.at[h, n]))
            high, low = split(tbuf[h, n])
            th[h, n] = high
            tl[h, n] = low

    landed(out, lsem.at[1])
    process(0)

    arrive(1)

    @pl.loop(1, 9)
    def _(i):
        @pl.when(i < 8)
        def _():
            whole(i)
            process(i)

        pass_on(i - 1)
        pl.when(i < 7)(lambda: arrive(i + 1))

    @pl.loop(0, 8)
    def _(i):
        rows = rows_of(piece(i))
        for n in (0, 1):
            for m in (0, 1):
                landed(rbuf.at[n, pl.ds(pl.multiple_of(rows.start + m * 128, 128), 128)], psem.at[n, m, i])
        out[rows, :] = out[rows, :] - (rbuf[0, rows] + rbuf[1, rows])
        pltpu.make_async_copy(out.at[rows], result.at[rows], osem.at[i]).start()

    for cp, when in sends:
        if when is None:
            cp.wait_send()
        else:
            pl.when(when)(lambda: cp.wait_send())

    @pl.when(k == 0)
    def _():
        remote(sbuf.at[z], sbuf.at[z], csend.at[0, 0], csem.at[0, 0], dev(x, y, z, 1)).wait_send()

    for q in (0, 1):
        ring(z, rsend.at[0, q], 1, q, z_up).wait_send()
        ring(z, rsend.at[8, q], 2, q, z_down).wait_send()

    @pl.loop(1, 8)
    def _(i):
        for q in (0, 1):
            cp, go = ring_on(z, i, q)
            pl.when(go)(lambda: cp.wait_send())
            to_sibling(z, i, q).wait_send()

    @pl.loop(0, 8)
    def _(i):
        for n, by in ups:
            relay_copy(i, n, by).wait_send()
            for m in (0, 1):
                partial_copy(i, n, by, m).wait_send()
        rows = rows_of(piece(i))
        pltpu.make_async_copy(out.at[rows], result.at[rows], osem.at[i]).wait()


def local(left_panel, upper_inverse, lower_inverse, top_panel, trailing):
    dma = pltpu.SemaphoreType.DMA
    return pl.pallas_call(
        kernel,
        out_shape=jax.ShapeDtypeStruct(trailing.shape, F32),
        in_specs=[pl.BlockSpec(memory_space=pl.ANY)] * 5,
        out_specs=pl.BlockSpec(memory_space=pl.ANY),
        scratch_shapes=[
            pltpu.VMEM((2048, 128), F32),
            pltpu.VMEM((8, B, B), F32),
            pltpu.VMEM((2048, B), F32),
            pltpu.VMEM((B, 2048), F32),
            pltpu.VMEM((4, 512, B), F32),
            pltpu.VMEM((4, B, 512), F32),
            pltpu.VMEM((8, 2, B, B), F32),
            pltpu.VMEM((2, B, B), F32),
            pltpu.VMEM((2, 2, B, B), F32),
            pltpu.VMEM((2, 2, B, B), BF16),
            pltpu.VMEM((2, 2, B, B), BF16),
            pltpu.VMEM((8, 4, B, 128), F32),
            pltpu.VMEM((2, 2048, 128), F32),
            pltpu.VMEM((2, 8, 128, 128), F32),
            dma((8,)), dma((3,)), dma((2, 3)), dma((4, 4, 2)), dma((4, 6)), dma((2, 2)), dma((4, 2)),
            dma((8, 2)), dma((9, 2)), dma((8, 2)), dma((8, 2)),
            dma((2, 8)), dma((2, 8)), dma((2, 2, 8)), dma((2, 2, 8)), dma((2,)), dma((8,)), pltpu.SemaphoreType.REGULAR,
        ],
        compiler_params=pltpu.CompilerParams(
            collective_id=0, has_side_effects=True, vmem_limit_bytes=60 * 2**20
        ),
        name="schur",
    )(left_panel, upper_inverse, lower_inverse, top_panel, trailing)


def solution(mesh):
    placed = (
        P(("row", "col"), "depth"),
        P(None, "depth"),
        P("depth", None),
        P("depth", "col"),
        P("row", ("col", "depth")),
    )
    return jax.shard_map(
        local, mesh=mesh, in_specs=placed, out_specs=P("row", ("col", "depth")), check_vma=False
    )
```

```python
import functools

import jax
import jax.numpy as jnp
from jax import lax
from jax.experimental import pallas as pl
from jax.experimental.pallas import tpu as pltpu
from jax.sharding import PartitionSpec as P

MESH = pl.DeviceIdType.MESH
F32 = jnp.float32
BF16 = jnp.bfloat16
B = 256


def split(v):
    high = v.astype(BF16)
    return high, (v - high.astype(F32)).astype(BF16)


def mm3(a, b):
    (ah, al), (bh, bl) = a, b
    dot = functools.partial(jnp.dot, preferred_element_type=F32)
    return dot(ah, bh) + (dot(ah, bl) + dot(al, bh))


def kernel(
    left, upper, lower, top, trailing, result,
    out, gbuf, uown, lown, ubuf, lbuf, sbuf, tloc, tbuf, th, tl, pbuf, rbuf, relay,
    gsem, xsend, gsend, fsem, fsend, tsem, tsend, rsem, rsend, csem, csend,
    esem, esend, psem, psend, lsem, osem, go,
):
    x = lax.axis_index("row")
    c = lax.axis_index("col")
    d = lax.axis_index("depth")
    k = lax.rem(c, 2)
    zl = c // 2
    y = lax.rem(d, 4)
    zh = d // 4
    z = zh * 4 + zl
    d2 = (1 - zh) * 4 + y

    def dev(x_, y_, z_, k_):
        return (x_, lax.rem(z_, 4) * 2 + k_, (z_ // 4) * 4 + y_)

    def rot4(v, by):
        return lax.rem(v + by + 4, 4)

    def rot8(v, by):
        return lax.rem(v + by + 8, 8)

    def remote(src, dst, ss, rs, device):
        return pltpu.make_async_remote_copy(
            src_ref=src, dst_ref=dst, send_sem=ss, recv_sem=rs, device_id=device, device_id_type=MESH
        )

    def landed(ref, sem):
        pltpu.make_async_copy(ref, ref, sem).wait()

    zo = rot8(z, 4)
    z_up, z_down = rot8(z, 1), rot8(z, -1)
    is0, is1 = k == 0, k == 1

    pl.when(is0)(lambda: pltpu.make_async_copy(upper, uown, lsem.at[0]).start())
    pl.when(is1)(lambda: pltpu.make_async_copy(lower, lown, lsem.at[0]).start())
    pltpu.make_async_copy(trailing, out, lsem.at[1]).start()

    is_self = jnp.logical_and(k == 0, zh == 0)
    pl.when(is_self)(lambda: pltpu.make_async_copy(left, gbuf.at[d], gsem.at[d]).start())
    kept = top.at[:, pl.ds(pl.multiple_of(zh * 512 + lax.rem(x, 2) * B, B), B)]
    pl.when(jnp.logical_and(is1, x // 2 == 1))(
        lambda: pltpu.make_async_copy(kept, gbuf.at[d], gsem.at[d]).start()
    )

    peers = [dev(x, y, z, 1 - k), dev(x, y, zo, 0), dev(x, y, zo, 1), dev(x, y, z_up, k), dev(x, y, z_down, k)]
    peers += [dev(x, rot4(y, i), z, k) for i in (1, 2, 3)]
    peers += [dev(rot4(x, i), y, z, j) for i in (1, 3) for j in (0, 1)]
    barrier = pltpu.get_barrier_semaphore()
    for peer in peers:
        pl.semaphore_signal(barrier, inc=1, device_id=peer, device_id_type=MESH)
    pl.semaphore_wait(barrier, len(peers))

    sends = []

    def start(cp, when=None):
        if when is None:
            cp.start()
        else:
            pl.when(when)(lambda: cp.start())
        sends.append((cp, when))

    def send_left(when):
        start(remote(left, gbuf.at[d], xsend.at[0], gsem.at[d], dev(x, y, k * 4 + zl, 0)), when)

    send_left(jnp.logical_and(k == zh, jnp.logical_not(is_self)))

    mine = k == x // 2
    for h in (0, 1):
        block = top.at[:, pl.ds(pl.multiple_of(h * 512 + lax.rem(x, 2) * B, B), B)]
        own = jnp.logical_and(k == 1, zh == h)
        start(
            remote(block, gbuf.at[d], xsend.at[1 + h], gsem.at[d], dev(x, y, h * 4 + zl, 1)),
            jnp.logical_and(mine, jnp.logical_not(own)),
        )

    edge = jnp.logical_or(zl == 0, zl == 3)
    z_cross = jnp.where(zl == 0, z_down, z_up)
    z_in = jnp.where(zl == 0, z_up, z_down)

    def u_share(g, xs, half=None):
        rows = pl.ds(xs * 128, 128) if half is None else pl.ds(xs * 128 + half * 64, 64)
        return ubuf.at[g, rows]

    def l_share(g, xs, half=None):
        rows = pl.ds(xs * 64, 64) if half is None else pl.ds(xs * 64 + half * 32, 32)
        return lbuf.at[g, rows]

    kinds = ((is0, u_share), (is1, l_share))
    def feed(g, kind):
        uq = upper.at[pl.ds(pl.multiple_of(g * 512 + x * 128, 128), 128), :]
        lq = lower.at[pl.ds(pl.multiple_of(x * 64, 64), 64), pl.ds(g * 512, 512)]
        is_k, share = kinds[kind]
        start(
            remote((uq, lq)[kind], share(g, x), fsend.at[g, 0], fsem.at[g, x, 0], dev(x, y, z_cross, k)),
            jnp.logical_and(jnp.logical_and(edge, is_k), 2 * g <= d),
        )

    def chunk(g):
        wanted = 2 * g <= d2

        @pl.when(wanted)
        def _():
            landed(u_share(g, x), fsem.at[g, x, 0])

        for is_k, share in kinds:
            go = jnp.logical_and(wanted, is_k)
            r = share(g, x)
            start(
                remote(r, r, fsend.at[g, 1], fsem.at[g, x, 0], dev(x, y, z_in, k)), jnp.logical_and(edge, go)
            )
            start(remote(r, r, fsend.at[g, 2], fsem.at[g, x, 0], dev(rot4(x, 1), y, z, k)), go)
            start(remote(r, r, fsend.at[g, 3], fsem.at[g, x, 0], dev(rot4(x, -1), y, z, k)), go)

    def chunk_relay(g):
        wanted = 2 * g <= d2
        for half, by in ((0, 1), (1, -1)):
            xs = rot4(x, -by)

            @pl.when(wanted)
            def _():
                landed(u_share(g, xs), fsem.at[g, xs, 0])

            for is_k, share in kinds:
                r = share(g, xs, half)
                start(
                    remote(r, r, fsend.at[g, 4 + half], fsem.at[g, xs, half], dev(rot4(x, by), y, z, k)),
                    jnp.logical_and(wanted, is_k),
                )

    def gather_y(slot, j):
        for i in (1, 2, 3):
            yy = rot4(y, i)
            start(
                remote(gbuf.at[slot], gbuf.at[slot], gsend.at[j, i - 1], gsem.at[slot], dev(x, yy, z, k)),
                jnp.logical_or(slot < 4, yy > y),
            )

    feed(0, 1)
    feed(1, 1)
    feed(2, 1)
    feed(3, 1)
    landed(gbuf.at[d], gsem.at[d])
    gather_y(d, 0)
    pl.when(is0)(lambda: pl.semaphore_wait(go, 1))
    send_left(jnp.logical_and(is0, zh == 1))
    feed(0, 0)
    feed(1, 0)
    feed(2, 0)
    feed(3, 0)
    chunk(0)
    pl.when(is1)(
        lambda: pl.semaphore_signal(go, inc=1, device_id=dev(x, y, z, 0), device_id_type=MESH)
    )
    send_left(jnp.logical_and(is1, zh == 0))
    chunk(1)
    chunk_relay(0)
    chunk(2)
    landed(gbuf.at[d2], gsem.at[d2])
    gather_y(d2, 1)
    chunk_relay(1)
    chunk(3)
    chunk_relay(2)
    chunk_relay(3)

    landed(uown, lsem.at[0])

    def wait_block(i):
        @pl.when(jnp.logical_and(lax.rem(i, 4) != y, i <= 4 + y))
        def _():
            landed(gbuf.at[i], gsem.at[i])

    def wait_chunk(i):
        g = i // 2
        xs = rot4(x, 2)

        @pl.when(jnp.logical_and(lax.rem(i, 2) == 0, i <= d2))
        def _():
            landed(u_share(g, xs, 0), fsem.at[g, xs, 0])
            landed(u_share(g, xs, 1), fsem.at[g, xs, 1])

    @pl.when(k == 0)
    def _():
        sbuf[z] = jnp.zeros((2, B, B), F32)

        @pl.loop(0, 8)
        def _(i):
            wait_block(i)

            @pl.when(i <= d)
            def _():
                f = uown[pl.ds(pl.multiple_of(i * B, B), B), :]
                sbuf[z, zh] += mm3(split(gbuf[i]), split(f))

        @pl.loop(0, 8)
        def _(i):
            wait_chunk(i)

            @pl.when(i <= d2)
            def _():
                f = ubuf[i // 2, pl.ds(pl.multiple_of(lax.rem(i, 2) * B, B), B), :]
                sbuf[z, 1 - zh] += mm3(split(gbuf[i]), split(f))

        remote(sbuf.at[z], sbuf.at[z], csend.at[0, 0], csem.at[0, 0], dev(x, y, z, 1)).start()

    t_core = x // 2
    t_slot = lax.rem(x, 2)

    @pl.when(k == 1)
    def _():
        tloc[...] = jnp.zeros((2, B, B), F32)

        @pl.loop(0, 8)
        def _(i):
            wait_block(i)

            @pl.when(i <= d)
            def _():
                f = lown[:, pl.ds(pl.multiple_of(i * B, B), B)]
                tloc[zh] += mm3(split(f), split(gbuf[i]))

        @pl.loop(0, 8)
        def _(i):
            wait_chunk(i)

            @pl.when(i <= d2)
            def _():
                f = lbuf[i // 2, :, pl.ds(pl.multiple_of(lax.rem(i, 2) * B, B), B)]
                tloc[1 - zh] += mm3(split(f), split(gbuf[i]))

    for i, by in enumerate((0, 1, -1)):
        own = jnp.logical_and(t_core == 1, i == 0)
        for n in (0, 1):
            start(
                remote(
                    tloc.at[n], tbuf.at[t_slot, n], tsend.at[i, n], tsem.at[t_slot, n], dev(rot4(x, by), y, z, t_core)
                ),
                jnp.logical_and(is1, jnp.logical_not(own)),
            )
    for n in (0, 1):
        pl.when(jnp.logical_and(is1, t_core == 1))(
            lambda: pltpu.make_async_copy(tloc.at[n], tbuf.at[t_slot, n], tsem.at[t_slot, n]).start()
        )

    rel = rot4(x, -2 * k)
    t_near = 1 - lax.rem(rel, 2)
    t_half = jnp.where(jnp.logical_or(rel == 0, rel == 3), 1, 0)
    r = tbuf.at[t_near, t_half]
    pass_t = remote(r, r, tsend.at[3, 0], tsem.at[t_near, t_half], dev(rot4(x, 1 - 2 * t_half), y, z, k))
    pl.when(is1)(lambda: landed(r, tsem.at[t_near, t_half]))
    start(pass_t, is1)

    def piece(i):
        s = (i + 1) // 2
        return rot8(z, jnp.where(lax.rem(i, 2) == 1, -s, s))

    def quarter(p, core, q):
        return sbuf.at[p, :, pl.ds(pl.multiple_of(core * 128 + q * 64, 64), 64), :]

    def ring(p, ss, i, q, z_):
        r = quarter(p, k, q)
        return remote(r, r, ss, rsem.at[i, q], dev(x, y, z_, k))

    def to_sibling(p, i, q):
        r = quarter(p, k, q)
        return remote(r, r, csend.at[i, q], csem.at[i, q], dev(x, y, z, 1 - k))

    def ring_on(p, i, q):
        odd = lax.rem(i, 2) == 1
        go = jnp.where(odd, i < 7 - 2 * q, i < 5 + 2 * q)
        return ring(p, rsend.at[i, q], jnp.minimum(i + 2, 7), q, jnp.where(odd, z_up, z_down)), go

    def arrive(i):
        p = piece(i)
        for q in (0, 1):
            landed(quarter(p, k, q), rsem.at[i, q])
            cp, go = ring_on(p, i, q)
            pl.when(go)(lambda: cp.start())
            to_sibling(p, i, q).start()

    def whole(i):
        for q in (0, 1):
            landed(quarter(piece(i), 1 - k, q), csem.at[i, q])

    def rows_of(p):
        return pl.ds(pl.multiple_of((2 * lax.rem(p, 4) + p // 4) * B, B), B)

    ups = ((0, 1), (1, -1))

    def relay_copy(i, n, by):
        r = pbuf.at[i, rot4(y, 2), pl.ds(n * 128, 128)]
        return remote(r, relay.at[n, i], esend.at[n, i], esem.at[n, i], dev(x, rot4(y, by), z, k))

    def partial_copy(i, n, by, m):
        yy = rot4(y, by)
        rows = pl.ds(pl.multiple_of(rows_of(piece(i)).start + m * 128, 128), 128)
        return remote(
            pbuf.at[i, yy, pl.ds(m * 128, 128)], rbuf.at[n, rows], psend.at[n, m, i], psem.at[n, m, i],
            dev(x, yy, z, k),
        )

    def process(i):
        rows = rows_of(piece(i))
        p = piece(i)
        a = split(jnp.concatenate([sbuf[p, 0], sbuf[p, 1]], axis=1))
        for n_h, h in enumerate((1 - y // 2, y // 2)):
            acc = mm3(a, (th[h].reshape(2 * B, B), tl[h].reshape(2 * B, B)))
            pbuf[i, 2 * h] = acc[:, :128]
            pbuf[i, 2 * h + 1] = acc[:, 128:]
            if n_h == 0:
                for n, by in ups:
                    relay_copy(i, n, by).start()
        for n, by in ups:
            partial_copy(i, n, by, 1 - n).start()
        out[rows, :] = out[rows, :] - pbuf[i, y]

    def pass_on(i):
        for n, by in ups:
            landed(relay.at[n, i], esem.at[n, i])
            yy = rot4(y, by)
            part = pl.ds(n * 128, 128)
            pbuf[i, yy, part] = pbuf[i, yy, part] + relay[n, i]
            partial_copy(i, n, by, n).start()

    @pl.when(k == 1)
    def _():
        landed(sbuf.at[z], csem.at[0, 0])

    for q in (0, 1):
        ring(z, rsend.at[0, q], 1, q, z_up).start()
        ring(z, rsend.at[8, q], 2, q, z_down).start()

    pl.when(is0)(lambda: landed(r, tsem.at[t_near, t_half]))
    start(pass_t, is0)
    for h in (0, 1):
        for n in (0, 1):
            here = jnp.logical_and(t_near == h, t_half == n)
            pl.when(jnp.logical_not(here))(lambda: landed(tbuf.at[h, n], tsem.at[h, n]))
            high, low = split(tbuf[h, n])
            th[h, n] = high
            tl[h, n] = low

    landed(out, lsem.at[1])
    process(0)

    arrive(1)

    @pl.loop(1, 9)
    def _(i):
        @pl.when(i < 8)
        def _():
            whole(i)
            process(i)

        pass_on(i - 1)
        pl.when(i < 7)(lambda: arrive(i + 1))

    @pl.loop(0, 8)
    def _(i):
        rows = rows_of(piece(i))
        for n in (0, 1):
            for m in (0, 1):
                landed(rbuf.at[n, pl.ds(pl.multiple_of(rows.start + m * 128, 128), 128)], psem.at[n, m, i])
        out[rows, :] = out[rows, :] - (rbuf[0, rows] + rbuf[1, rows])
        pltpu.make_async_copy(out.at[rows], result.at[rows], osem.at[i]).start()

    for cp, when in sends:
        if when is None:
            cp.wait_send()
        else:
            pl.when(when)(lambda: cp.wait_send())

    @pl.when(k == 0)
    def _():
        remote(sbuf.at[z], sbuf.at[z], csend.at[0, 0], csem.at[0, 0], dev(x, y, z, 1)).wait_send()

    for q in (0, 1):
        ring(z, rsend.at[0, q], 1, q, z_up).wait_send()
        ring(z, rsend.at[8, q], 2, q, z_down).wait_send()

    @pl.loop(1, 8)
    def _(i):
        for q in (0, 1):
            cp, go = ring_on(z, i, q)
            pl.when(go)(lambda: cp.wait_send())
            to_sibling(z, i, q).wait_send()

    @pl.loop(0, 8)
    def _(i):
        for n, by in ups:
            relay_copy(i, n, by).wait_send()
            for m in (0, 1):
                partial_copy(i, n, by, m).wait_send()
        rows = rows_of(piece(i))
        pltpu.make_async_copy(out.at[rows], result.at[rows], osem.at[i]).wait()


def local(left_panel, upper_inverse, lower_inverse, top_panel, trailing):
    dma = pltpu.SemaphoreType.DMA
    return pl.pallas_call(
        kernel,
        out_shape=jax.ShapeDtypeStruct(trailing.shape, F32),
        in_specs=[pl.BlockSpec(memory_space=pl.ANY)] * 5,
        out_specs=pl.BlockSpec(memory_space=pl.ANY),
        scratch_shapes=[
            pltpu.VMEM((2048, 128), F32),
            pltpu.VMEM((8, B, B), F32),
            pltpu.VMEM((2048, B), F32),
            pltpu.VMEM((B, 2048), F32),
            pltpu.VMEM((4, 512, B), F32),
            pltpu.VMEM((4, B, 512), F32),
            pltpu.VMEM((8, 2, B, B), F32),
            pltpu.VMEM((2, B, B), F32),
            pltpu.VMEM((2, 2, B, B), F32),
            pltpu.VMEM((2, 2, B, B), BF16),
            pltpu.VMEM((2, 2, B, B), BF16),
            pltpu.VMEM((8, 4, B, 128), F32),
            pltpu.VMEM((2, 2048, 128), F32),
            pltpu.VMEM((2, 8, 128, 128), F32),
            dma((8,)), dma((3,)), dma((2, 3)), dma((4, 4, 2)), dma((4, 6)), dma((2, 2)), dma((4, 2)),
            dma((8, 2)), dma((9, 2)), dma((8, 2)), dma((8, 2)),
            dma((2, 8)), dma((2, 8)), dma((2, 2, 8)), dma((2, 2, 8)), dma((2,)), dma((8,)), pltpu.SemaphoreType.REGULAR,
        ],
        compiler_params=pltpu.CompilerParams(
            collective_id=0, has_side_effects=True, vmem_limit_bytes=60 * 2**20
        ),
        name="schur",
    )(left_panel, upper_inverse, lower_inverse, top_panel, trailing)


def solution(mesh):
    placed = (
        P(("row", "col"), "depth"),
        P(None, "depth"),
        P("depth", None),
        P("depth", "col"),
        P("row", ("col", "depth")),
    )
    return jax.shard_map(
        local, mesh=mesh, in_specs=placed, out_specs=P("row", ("col", "depth")), check_vma=False
    )
```
